256 devices in a mesh: px: 8 (over y, core), py: 32 (over z, x).
Axes of the slice: x: 4, y: 4, z: 8, core: 2. Of those that a mesh axis runs over, the one named last changes fastest.
Arguments:
- white_noise: float32 [512, 512, 512], P(('px', 'py')), may hold values from -6 to 6
- mode_amplitude: bfloat16 [512, 512, 512], P(('px', 'py')), may hold values from 0.099609375 to 0.59765625
- kick_noise: bfloat16 [512, 512, 512], P(('px', 'py')), may hold values from -6 to 6
- shell_owner: int32 [8, 32, 4096], P('px', 'py'), may hold values from 0 to 31, as said below
- galaxy_counts: int32 [8, 32, 32, 256, 128], P('px', 'py'), may hold values from 0 to 7
- shell_bias: float32 [8, 32], replicated, may hold values from 1 to 2
- shell_density: float32 [8, 32], replicated, may hold values from 2 to 4
- accepted: int32 [64], replicated, may hold values from 0 to 1
Outputs:
- log_gradient: float32 [512, 512, 512], P(('px', 'py'))
- next_state: float32 [512, 512, 512], P(('px', 'py'))
The draws below stay inside these ranges and needn't reach their ends.
Inputs may be any that keep to these rules, and one draw needn't show every extreme that they name: `shell_owner`: in every row a, one owner receives exactly 256 blocks from every device (a, b); each device's other blocks are spread over the other 31 owners of its row with loads that differ by at most one; so no device assigns more than 256 blocks to one owner.
All inputs are finite; a program needn't handle non-finite values.
Results may differ from the reference program's by a relative error of at most 0.0003.
Values sent between devices are 32-bit elements; how exact they have to be, the bound alone decides.
No kernel may reach another device: no remote copies, remote signals or barrier semaphores. Data moves between devices by JAX's collectives and lax.ppermute only.
A program may use at most 128 MiB of HBM per device.

```python
import math
import jax
import jax.numpy as jnp
from jax import lax

NX = 512
NY = 512
NZ = 512
BLOCK = 128
HISTORY = 64
XL = 64
YL = 16
BLK = 4096
CAP = 256
N_PX = 8
N_PY = 32


def draw_shell_owner(key, part):
    heavy = jax.random.randint(jax.random.fold_in(key, 11), (N_PX,), 0, N_PY)
    offset = jax.random.randint(jax.random.fold_in(key, 12), (N_PX * N_PY,), 0, N_PY - 1)
    keys = jax.random.split(jax.random.fold_in(key, 13), N_PX * N_PY)
    place = jnp.arange(BLK, dtype=jnp.int32)
    others = (place - CAP) % (N_PY - 1)

    def one_device(heavy_one, offset_one, key_one):
        rest = (heavy_one + 1 + (others + offset_one) % (N_PY - 1)) % N_PY
        line = jnp.where(place < CAP, heavy_one, rest)
        return jax.random.permutation(key_one, line)
    heavy_flat = jnp.repeat(heavy, N_PY)
    owners_flat = jax.vmap(one_device)(heavy_flat, offset, keys)
    return owners_flat.reshape(N_PX, N_PY, BLK).astype(jnp.int32)


def with_ends(array, rng, least, largest):
    dims = array.shape
    spot = [jax.random.randint(jax.random.fold_in(rng, axis), (), 0, dims[axis]) for axis in range(len(dims))]
    array = array.at[tuple(spot)].set(least)
    longest = dims.index(max(dims))
    spot[longest] = (spot[longest] + 1) % dims[longest]
    return array.at[tuple(spot)].set(largest)


def block_levels(own_key, shape, cuts, least, largest):
    factor_of = 1.0
    for axis_at, parts in cuts:
        heights = jax.random.uniform(jax.random.fold_in(jax.random.fold_in(own_key, 6), axis_at), (parts,), jnp.float32, least / len(cuts), largest / len(cuts))
        factor_of = factor_of * jnp.repeat(jnp.exp(heights), shape[axis_at] // parts).reshape((-1,) + (1,) * (len(shape) - 1 - axis_at))
    return factor_of


def scatter_about(key, extent, deviation, reach, cuts=(), kind=jnp.bfloat16):
    entries = jax.random.normal(key, extent, jnp.float32) * deviation
    if len(cuts) > 0:
        entries = block_levels(key, extent, cuts, -0.22, 0.18) * entries
    return jnp.clip(entries, min=-reach, max=reach).astype(kind)


def setup_inputs(seed: int = 0) -> dict:
    arg_keys = jax.random.split(jax.random.key(seed), 9)
    return {
        "white_noise": scatter_about(arg_keys[0], (NZ, NX, NY), 1.0, 6.0, ((0, 256),), jnp.float32),
        "mode_amplitude": jnp.clip(jnp.exp(math.log(0.59765625) - 1.7917595 * jax.random.uniform(arg_keys[1], (NZ, NX, NY), jnp.float32) ** block_levels(arg_keys[1], (NZ, NX, NY), ((0, 256),), -0.2, 0.2)), 0.099609375, 0.59765625).astype(jnp.bfloat16),
        "kick_noise": scatter_about(arg_keys[2], (NZ, NX, NY), 1.0, 6.0, ((0, 256),)),
        "shell_owner": draw_shell_owner(jax.random.fold_in(arg_keys[8], 71), 0),
        "galaxy_counts": with_ends(jax.random.randint(arg_keys[4], (N_PX, N_PY, N_PY, CAP, BLOCK), 0, 8), jax.random.fold_in(arg_keys[4], 1), 0, 7).astype(jnp.int32),
        "shell_bias": jnp.clip(jax.random.uniform(arg_keys[5], (N_PX, N_PY), jnp.float32, 1.0, 2.0), 1.0, 2.0),
        "shell_density": jnp.clip(jnp.exp(jax.random.uniform(arg_keys[6], (N_PX, N_PY), jnp.float32, math.log(2.0), math.log(4.0))), 2.0, 4.0),
        "accepted": with_ends(jax.random.randint(arg_keys[7], (HISTORY,), 0, 2), jax.random.fold_in(arg_keys[7], 1), 0, 1).astype(jnp.int32),
    }


HIGHEST = lax.Precision.HIGHEST

def hartley_table(rows_in, cols_in, order):
    angle_index = rows_in[:, None] * cols_in[None, :] % order
    angle = angle_index.astype(jnp.float32) * (2.0 * math.pi / order)
    return jnp.cos(angle) + jnp.sin(angle)

def adapted_step(accepted):
    powers = jnp.power(jnp.float32(0.9), jnp.arange(accepted.shape[0], dtype=jnp.int32).astype(jnp.float32))
    accept_rate = jnp.float32(0.1) * jnp.sum(accepted.astype(jnp.float32) * powers)
    return jnp.float32(0.02) * jnp.exp(jnp.float32(2.0) * (accept_rate - jnp.float32(0.574)))

def reference(white_noise, mode_amplitude, kick_noise, shell_owner, galaxy_counts, shell_bias, shell_density, accepted):
    span_x = jnp.arange(NX, dtype=jnp.int32)
    span_y = jnp.arange(NY, dtype=jnp.int32)
    span_z = jnp.arange(NZ, dtype=jnp.int32)
    table_x = hartley_table(span_x, span_x, NX)
    table_y = hartley_table(span_y, span_y, NY)
    table_z = hartley_table(span_z, span_z, NZ)
    scale_x = 1.0 / math.sqrt(NX)
    scale_y = 1.0 / math.sqrt(NY)
    scale_z = 1.0 / math.sqrt(NZ)
    amplitude_live = mode_amplitude.astype(jnp.float32).at[0, 0, 0].set(0.0)
    weighted = amplitude_live * white_noise
    first_pass = jnp.einsum('zxk,ky->zxy', weighted, table_y, precision=HIGHEST) * scale_y
    second_pass = jnp.einsum('zky,kx->zxy', first_pass, table_x, precision=HIGHEST) * scale_x
    contrast = jnp.einsum('kxy,kz->xyz', second_pass, table_z, precision=HIGHEST) * scale_z
    blocks = contrast.reshape(N_PX, XL, N_PY, YL, NZ // BLOCK, BLOCK)
    blocks = blocks.transpose(0, 2, 1, 3, 4, 5).reshape(N_PX, N_PY, BLK, BLOCK)
    onehot = (shell_owner[..., None] == jnp.arange(N_PY, dtype=jnp.int32)).astype(jnp.int32)
    rank_index = lax.optimization_barrier(jnp.sum(jnp.cumsum(onehot, axis=2) * onehot, axis=3)) - 1
    row_index = jnp.arange(N_PX, dtype=jnp.int32)[:, None, None]
    col_index = jnp.arange(N_PY, dtype=jnp.int32)[None, :, None]
    galaxy = galaxy_counts[row_index, shell_owner, col_index, rank_index].astype(jnp.float32)
    block_bias = shell_bias[row_index, shell_owner][..., None]
    block_density = shell_density[row_index, shell_owner][..., None]
    like_grad = block_bias * (galaxy - block_density * jnp.exp(block_bias * blocks))
    like_grad = like_grad.reshape(N_PX, N_PY, XL, YL, NZ).transpose(0, 2, 1, 3, 4).reshape(NX, NY, NZ)
    back_z = jnp.einsum('xyz,zk->kxy', like_grad, table_z, precision=HIGHEST) * scale_z
    back_x = jnp.einsum('kxy,xq->kqy', back_z, table_x, precision=HIGHEST) * scale_x
    back_y = jnp.einsum('kqy,yp->kqp', back_x, table_y, precision=HIGHEST) * scale_y
    log_gradient = amplitude_live * back_y - white_noise
    step_size = adapted_step(accepted)
    next_state = white_noise + step_size * log_gradient + jnp.sqrt(2.0 * step_size) * kick_noise.astype(jnp.float32)
    return (log_gradient, next_state)
```

```python
import math

import jax
import jax.numpy as jnp
import numpy as np
from jax import lax
from jax.experimental import pallas as pl
from jax.experimental.pallas import tpu as pltpu
from jax.sharding import PartitionSpec as P

BLOCK = 128
HALF = BLOCK // 2
VMEM_BYTES = 56 * 1024 * 1024


def scaled_table(rows, cols, order):
    angle = (rows[:, None] * cols[None, :] % order).astype(np.float64) * (2.0 * math.pi / order)
    table = ((np.cos(angle) + np.sin(angle)) / math.sqrt(order)).astype(np.float32)
    high = table.astype(jnp.bfloat16)
    low = (table - high.astype(np.float32)).astype(jnp.bfloat16)
    return high, low


def split(value):
    high = value.astype(jnp.bfloat16)
    low = (value - high.astype(jnp.float32)).astype(jnp.bfloat16)
    return high, low


def product(left, right, contract=((1,), (0,))):
    left_high, left_low = left
    right_high, right_low = right
    dot = lambda a, b: lax.dot_general(a, b, (contract, ((), ())), preferred_element_type=jnp.float32)
    return dot(left_high, right_high) + (dot(left_high, right_low) + dot(left_low, right_high))


def first_half(shape):
    return lax.broadcasted_iota(jnp.int32, shape, len(shape) - 1) % BLOCK < HALF


def live_amplitude(first_ref, amplitude_ref):
    amplitude = amplitude_ref[0].astype(jnp.float32)
    rows = lax.broadcasted_iota(jnp.int32, amplitude.shape, 0)
    cols = lax.broadcasted_iota(jnp.int32, amplitude.shape, 1)
    anchor = (rows + cols + first_ref[0] + pl.program_id(0)) == 0
    return jnp.where(anchor, 0.0, amplitude)


def synthesis_kernel(
    first_ref, white_ref, amplitude_ref, y_high, y_low, even_high, even_low, odd_high, odd_low, out_ref
):
    weighted = split(live_amplitude(first_ref, amplitude_ref) * white_ref[0])
    passed = product((y_high[...], y_low[...]), weighted, ((1,), (1,)))
    rows = passed.shape[0] // 2
    lower = product(split(passed[:rows]), (even_high[...], even_low[...]))
    upper = product(split(passed[rows:]), (odd_high[...], odd_low[...]))
    groups = out_ref.shape[1]
    for pair in range(out_ref.shape[0] // 2):
        left = lower[:, pair * BLOCK : (pair + 1) * BLOCK]
        right = upper[:, pair * BLOCK : (pair + 1) * BLOCK]
        mask = first_half(left.shape)
        out_ref[2 * pair, :, 0] = jnp.where(mask, left, right).reshape(groups, -1, BLOCK)
        out_ref[2 * pair + 1, :, 0] = jnp.where(mask, right, left).reshape(groups, -1, BLOCK)


def shell_kernel(field_ref, galaxy_ref, bias_ref, density_ref, z_high, z_low, out_ref):
    table = (z_high[...], z_low[...])
    size_z = z_high.shape[0]
    rows_y = field_ref.shape[0] // size_z
    for step in range(rows_y // 2):
        field = jnp.concatenate(
            [field_ref[pl.ds(2 * step + k, size_z, stride=rows_y), :] for k in range(2)], axis=1
        )
        contrast = product(table, split(field))
        span = slice(2 * step * BLOCK, 2 * (step + 1) * BLOCK)
        grads = []
        for quarter in range(size_z // BLOCK):
            depth = slice(quarter * BLOCK, (quarter + 1) * BLOCK)
            bias = bias_ref[quarter : quarter + 1, span]
            density = density_ref[quarter : quarter + 1, span]
            grads.append(bias * (galaxy_ref[depth, span] - density * jnp.exp(bias * contrast[depth])))
        back = product(table, split(jnp.concatenate(grads, axis=0)))
        for k in range(2):
            out_ref[pl.ds(2 * step + k, size_z, stride=rows_y), :] = back[:, k * BLOCK : (k + 1) * BLOCK]


def analysis_kernel(
    first_ref, step_ref, field_ref, white_ref, amplitude_ref, kick_ref,
    y_high, y_low, even_high, even_low, odd_high, odd_low, grad_ref, next_ref,
):
    lower, upper = [], []
    for pair in range(field_ref.shape[0] // 2):
        left = field_ref[2 * pair, :, 0].reshape(-1, BLOCK)
        right = field_ref[2 * pair + 1, :, 0].reshape(-1, BLOCK)
        mask = first_half(left.shape)
        lower.append(jnp.where(mask, left, right))
        upper.append(jnp.where(mask, right, left))
    contract = ((1,), (1,))
    lower = product(split(jnp.concatenate(lower, axis=1)), (even_high[...], even_low[...]), contract)
    upper = product(split(jnp.concatenate(upper, axis=1)), (odd_high[...], odd_low[...]), contract)
    passed = split(jnp.concatenate([lower, upper], axis=0))
    back = product(passed, (y_high[...], y_low[...]), ((0,), (0,)))
    white = white_ref[0]
    gradient = live_amplitude(first_ref, amplitude_ref) * back - white
    grad_ref[0] = gradient
    next_ref[0] = white + step_ref[0] * gradient + step_ref[1] * kick_ref[0].astype(jnp.float32)


def adapted_step(accepted):
    powers = jnp.power(
        jnp.float32(0.9), jnp.arange(accepted.shape[0], dtype=jnp.int32).astype(jnp.float32)
    )
    accept_rate = jnp.float32(0.1) * jnp.sum(accepted.astype(jnp.float32) * powers)
    return jnp.float32(0.02) * jnp.exp(jnp.float32(2.0) * (accept_rate - jnp.float32(0.574)))


def solution(mesh):
    rows_px, rows_py = mesh.shape["px"], mesh.shape["py"]
    devices = rows_px * rows_py

    def body(
        white_noise, mode_amplitude, kick_noise, shell_owner, galaxy_counts, shell_bias, shell_density, accepted
    ):
        depth, size_x, size_y = white_noise.shape
        size_z = depth * devices
        span_x, span_y = size_x // rows_px, size_y // rows_py
        rows_y = span_y // 2
        quarters = size_z // BLOCK
        row_index = lax.axis_index("px")
        col_index = lax.axis_index("py")
        first = ((row_index * rows_py + col_index) * depth).reshape(1)

        plain_x, plain_y, plain_z = np.arange(size_x), np.arange(size_y), np.arange(size_z)
        y_order = plain_y.reshape(rows_py, 2, rows_y).transpose(1, 0, 2).reshape(-1)
        x_order = plain_x.reshape(-1, 2, HALF)[:, ::-1].reshape(-1)
        y_table = scaled_table(y_order, plain_y, size_y)
        even_table = scaled_table(plain_x, plain_x, size_x)
        odd_table = scaled_table(plain_x, x_order, size_x)
        z_table = scaled_table(plain_z, plain_z, size_z)
        tables = [jnp.asarray(part) for part in (*y_table, *even_table, *odd_table)]

        capacity = galaxy_counts.shape[3]
        counts = lax.all_to_all(galaxy_counts[0, 0], "py", split_axis=0, concat_axis=0, tiled=True)

        owner_list = shell_owner.reshape(-1)
        peers = jnp.arange(rows_py, dtype=jnp.int32)
        onehot = owner_list[:, None] == peers[None, :]
        onehot_int = onehot.astype(jnp.int32)
        rank_index = jnp.sum(jnp.cumsum(onehot_int, axis=0) * onehot_int, axis=1) - 1
        slot_index = owner_list * capacity + rank_index
        bias_row = lax.dynamic_index_in_dim(shell_bias, row_index, 0, keepdims=False)
        density_row = lax.dynamic_index_in_dim(shell_density, row_index, 0, keepdims=False)

        def by_column(blocks):
            grid = blocks.reshape(span_x, 2, rows_y, quarters)
            grid = jnp.where(row_index % 2 == 0, grid, grid[:, ::-1])
            return grid.transpose(3, 2, 1, 0).reshape(quarters, -1)

        slot_grid = by_column(slot_index)
        owner_grid = by_column(owner_list)
        hit = owner_grid[:, :, None] == peers
        bias_grid = jnp.sum(jnp.where(hit, bias_row, 0.0), axis=-1)
        density_grid = jnp.sum(jnp.where(hit, density_row, 0.0), axis=-1)

        whole = lambda array: pl.BlockSpec(array.shape, lambda i: (0,) * array.ndim)
        plane = pl.BlockSpec((1, size_x, size_y), lambda i: (i, 0, 0))
        scalar = pl.BlockSpec(memory_space=pltpu.SMEM)
        packed_shape = (rows_px, rows_py, depth, rows_y, BLOCK)
        packed = pl.BlockSpec((rows_px, rows_py, 1, rows_y, BLOCK), lambda i: (0, 0, i, 0, 0))
        params = pltpu.CompilerParams(vmem_limit_bytes=VMEM_BYTES)

        flops = 2 * 3 * 2 * depth * size_x * size_y * size_x
        sent = pl.pallas_call(
            synthesis_kernel,
            grid=(depth,),
            in_specs=[scalar, plane, plane] + [whole(table) for table in tables],
            out_specs=packed,
            out_shape=jax.ShapeDtypeStruct(packed_shape, jnp.float32),
            compiler_params=params,
            cost_estimate=pl.CostEstimate(flops=flops, bytes_accessed=8 * 2**20, transcendentals=0),
            name="synthesis",
        )(first, white_noise, mode_amplitude, *tables)

        chunk = depth * rows_y
        field = lax.all_to_all(
            sent.reshape(devices, chunk, BLOCK), ("px", "py"), split_axis=0, concat_axis=0, tiled=True
        )

        picked = counts.reshape(-1, BLOCK).at[slot_grid.reshape(-1)].get(mode="promise_in_bounds")
        galaxy = picked.reshape(quarters, -1, BLOCK).transpose(0, 2, 1).reshape(size_z, -1).astype(jnp.float32)

        back = pl.pallas_call(
            shell_kernel,
            out_shape=jax.ShapeDtypeStruct((size_z * rows_y, BLOCK), jnp.float32),
            compiler_params=params,
            cost_estimate=pl.CostEstimate(flops=flops, bytes_accessed=8 * 2**20, transcendentals=size_z * 1024),
            name="shell_gradient",
        )(field.reshape(-1, BLOCK), galaxy, bias_grid, density_grid, *[jnp.asarray(part) for part in z_table])

        returned = lax.all_to_all(
            back.reshape(devices, chunk, BLOCK), ("px", "py"), split_axis=0, concat_axis=0, tiled=True
        )
        step_size = adapted_step(accepted)
        steps = jnp.stack([step_size, jnp.sqrt(2.0 * step_size)])
        out_plane = jax.ShapeDtypeStruct(white_noise.shape, jnp.float32)
        return pl.pallas_call(
            analysis_kernel,
            grid=(depth,),
            in_specs=[scalar, scalar, packed, plane, plane, plane] + [whole(table) for table in tables],
            out_specs=(plane, plane),
            out_shape=(out_plane, out_plane),
            compiler_params=params,
            cost_estimate=pl.CostEstimate(flops=flops, bytes_accessed=12 * 2**20, transcendentals=0),
            name="analysis",
        )(first, steps, returned.reshape(packed_shape), white_noise, mode_amplitude, kick_noise, *tables)

    modes = P(("px", "py"), None, None)
    return jax.shard_map(
        body,
        mesh=mesh,
        in_specs=(modes, modes, modes, P("px", "py", None), P("px", "py", None, None, None), P(), P(), P()),
        out_specs=(modes, modes),
        check_vma=False,
    )
```

```python
import math

import jax
import jax.numpy as jnp
import numpy as np
from jax import lax
from jax.experimental import pallas as pl
from jax.experimental.pallas import tpu as pltpu
from jax.sharding import PartitionSpec as P

BLOCK = 128
HALF = BLOCK // 2
WIDTH = 4
VMEM_BYTES = 56 * 1024 * 1024


def scaled_table(rows, cols, order):
    angle = (rows[:, None] * cols[None, :] % order).astype(np.float64) * (2.0 * math.pi / order)
    table = ((np.cos(angle) + np.sin(angle)) / math.sqrt(order)).astype(np.float32)
    high = table.astype(jnp.bfloat16)
    low = (table - high.astype(np.float32)).astype(jnp.bfloat16)
    return high, low


def split(value):
    high = value.astype(jnp.bfloat16)
    low = (value - high.astype(jnp.float32)).astype(jnp.bfloat16)
    return high, low


def product(left, right, contract=((1,), (0,))):
    left_high, left_low = left
    right_high, right_low = right
    dot = lambda a, b: lax.dot_general(a, b, (contract, ((), ())), preferred_element_type=jnp.float32)
    return dot(left_high, right_high) + (dot(left_high, right_low) + dot(left_low, right_high))


def first_half(shape):
    return lax.broadcasted_iota(jnp.int32, shape, len(shape) - 1) % BLOCK < HALF


def live_amplitude(first_ref, amplitude_ref):
    amplitude = amplitude_ref[0].astype(jnp.float32)
    rows = lax.broadcasted_iota(jnp.int32, amplitude.shape, 0)
    cols = lax.broadcasted_iota(jnp.int32, amplitude.shape, 1)
    anchor = (rows + cols + first_ref[0] + pl.program_id(0)) == 0
    return jnp.where(anchor, 0.0, amplitude)


def synthesis_kernel(
    first_ref, white_ref, amplitude_ref, y_high, y_low, even_high, even_low, odd_high, odd_low, out_ref
):
    weighted = split(live_amplitude(first_ref, amplitude_ref) * white_ref[0])
    passed = product((y_high[...], y_low[...]), weighted, ((1,), (1,)))
    rows = passed.shape[0] // 2
    lower = product(split(passed[:rows]), (even_high[...], even_low[...]))
    upper = product(split(passed[rows:]), (odd_high[...], odd_low[...]))
    groups = out_ref.shape[1]
    for pair in range(out_ref.shape[0] // 2):
        left = lower[:, pair * BLOCK : (pair + 1) * BLOCK]
        right = upper[:, pair * BLOCK : (pair + 1) * BLOCK]
        mask = first_half(left.shape)
        out_ref[2 * pair, :, 0] = jnp.where(mask, left, right).reshape(groups, -1, BLOCK)
        out_ref[2 * pair + 1, :, 0] = jnp.where(mask, right, left).reshape(groups, -1, BLOCK)


def shell_kernel(field_ref, galaxy_ref, bias_ref, density_ref, z_high, z_low, out_ref):
    table = (z_high[...], z_low[...])
    size_z = z_high.shape[0]
    rows_y = field_ref.shape[0] // size_z
    for step in range(rows_y // 2):
        field = jnp.concatenate(
            [field_ref[pl.ds(2 * step + k, size_z, stride=rows_y), :] for k in range(2)], axis=1
        )
        contrast = product(table, split(field))
        span = slice(2 * step * BLOCK, 2 * (step + 1) * BLOCK)
        grads = []
        for quarter in range(size_z // BLOCK):
            depth = slice(quarter * BLOCK, (quarter + 1) * BLOCK)
            bias = bias_ref[quarter : quarter + 1, span]
            density = density_ref[quarter : quarter + 1, span]
            grads.append(bias * (galaxy_ref[depth, span] - density * jnp.exp(bias * contrast[depth])))
        back = product(table, split(jnp.concatenate(grads, axis=0)))
        for k in range(2):
            out_ref[pl.ds(2 * step + k, size_z, stride=rows_y), :] = back[:, k * BLOCK : (k + 1) * BLOCK]


def analysis_kernel(
    first_ref, step_ref, field_ref, white_ref, amplitude_ref, kick_ref,
    y_high, y_low, even_high, even_low, odd_high, odd_low, grad_ref, next_ref,
):
    lower, upper = [], []
    for pair in range(field_ref.shape[0] // 2):
        left = field_ref[2 * pair, :, 0].reshape(-1, BLOCK)
        right = field_ref[2 * pair + 1, :, 0].reshape(-1, BLOCK)
        mask = first_half(left.shape)
        lower.append(jnp.where(mask, left, right))
        upper.append(jnp.where(mask, right, left))
    contract = ((1,), (1,))
    lower = product(split(jnp.concatenate(lower, axis=1)), (even_high[...], even_low[...]), contract)
    upper = product(split(jnp.concatenate(upper, axis=1)), (odd_high[...], odd_low[...]), contract)
    passed = split(jnp.concatenate([lower, upper], axis=0))
    back = product(passed, (y_high[...], y_low[...]), ((0,), (0,)))
    white = white_ref[0]
    gradient = live_amplitude(first_ref, amplitude_ref) * back - white
    grad_ref[0] = gradient
    next_ref[0] = white + step_ref[0] * gradient + step_ref[1] * kick_ref[0].astype(jnp.float32)


def adapted_step(accepted):
    powers = jnp.power(
        jnp.float32(0.9), jnp.arange(accepted.shape[0], dtype=jnp.int32).astype(jnp.float32)
    )
    accept_rate = jnp.float32(0.1) * jnp.sum(accepted.astype(jnp.float32) * powers)
    return jnp.float32(0.02) * jnp.exp(jnp.float32(2.0) * (accept_rate - jnp.float32(0.574)))


def heavy_ranks(counts, keep, heavy, col_index):
    size, capacity, block = counts.shape
    height = size // WIDTH
    parts = counts.reshape(height, WIDTH, capacity, block)
    at_z, at_x = col_index // WIDTH, col_index % WIDTH
    heavy_z, heavy_x = heavy // WIDTH, heavy % WIDTH

    def pick(array, axis, index):
        return lax.dynamic_index_in_dim(array, index, axis, keepdims=False)

    def column(index):
        part = lax.dynamic_slice(parts, (0, index, keep, 0), (height, 1, capacity - keep, block))
        return part.reshape(height, capacity - keep, block)

    mine = column(at_x)
    for shift in range(1, WIDTH):
        pairs = [(i, i // WIDTH * WIDTH + (i + shift) % WIDTH) for i in range(size)]
        arrived = lax.ppermute(column((at_x + shift) % WIDTH), "py", pairs)
        mine = jnp.where((at_x - heavy_x) % WIDTH == shift, arrived, mine)
    bit = 1
    while bit < height:
        mine = mine.reshape(height // (2 * bit), 2, *mine.shape[1:])
        here = at_z // bit % 2
        pairs = [(i, i ^ (bit * WIDTH)) for i in range(size)]
        arrived = lax.ppermute(pick(mine, 1, 1 - here), "py", pairs)
        mine = jnp.where(here == heavy_z // bit % 2, pick(mine, 1, here), arrived)
        bit *= 2
    return mine.reshape(capacity - keep, block)


def solution(mesh):
    rows_px, rows_py = mesh.shape["px"], mesh.shape["py"]
    devices = rows_px * rows_py

    def body(
        white_noise, mode_amplitude, kick_noise, shell_owner, galaxy_counts, shell_bias, shell_density, accepted
    ):
        depth, size_x, size_y = white_noise.shape
        size_z = depth * devices
        span_x, span_y = size_x // rows_px, size_y // rows_py
        rows_y = span_y // 2
        quarters = size_z // BLOCK
        row_index = lax.axis_index("px")
        col_index = lax.axis_index("py")
        first = ((row_index * rows_py + col_index) * depth).reshape(1)

        plain_x, plain_y, plain_z = np.arange(size_x), np.arange(size_y), np.arange(size_z)
        y_order = plain_y.reshape(rows_py, 2, rows_y).transpose(1, 0, 2).reshape(-1)
        x_order = plain_x.reshape(-1, 2, HALF)[:, ::-1].reshape(-1)
        y_table = scaled_table(y_order, plain_y, size_y)
        even_table = scaled_table(plain_x, plain_x, size_x)
        odd_table = scaled_table(plain_x, x_order, size_x)
        z_table = scaled_table(plain_z, plain_z, size_z)
        tables = [jnp.asarray(part) for part in (*y_table, *even_table, *odd_table)]

        galaxy_in = galaxy_counts[0, 0]
        blocks, capacity = shell_owner.shape[-1], galaxy_counts.shape[3]
        keep = -(-(-(-(blocks - capacity) // (rows_py - 1))) // 8) * 8
        owner_list = shell_owner.reshape(-1)
        peers = jnp.arange(rows_py, dtype=jnp.int32)
        onehot = owner_list[:, None] == peers[None, :]
        onehot_int = onehot.astype(jnp.int32)
        rank_index = jnp.sum(jnp.cumsum(onehot_int, axis=0) * onehot_int, axis=1) - 1
        heavy = jnp.argmax(jnp.sum(onehot_int, axis=0)).astype(jnp.int32)
        slot_index = jnp.where(
            rank_index < keep, owner_list * keep + rank_index, rows_py * keep + rank_index - keep
        )
        counts = lax.all_to_all(galaxy_in[:, :keep], "py", split_axis=0, concat_axis=0, tiled=True)
        extra = heavy_ranks(galaxy_in, keep, heavy, col_index)
        bias_row = lax.dynamic_index_in_dim(shell_bias, row_index, 0, keepdims=False)
        density_row = lax.dynamic_index_in_dim(shell_density, row_index, 0, keepdims=False)

        def by_column(blocks):
            grid = blocks.reshape(span_x, 2, rows_y, quarters)
            grid = jnp.where(row_index % 2 == 0, grid, grid[:, ::-1])
            return grid.transpose(3, 2, 1, 0).reshape(quarters, -1)

        slot_grid = by_column(slot_index)
        owner_grid = by_column(owner_list)
        hit = owner_grid[:, :, None] == peers
        bias_grid = jnp.sum(jnp.where(hit, bias_row, 0.0), axis=-1)
        density_grid = jnp.sum(jnp.where(hit, density_row, 0.0), axis=-1)

        whole = lambda array: pl.BlockSpec(array.shape, lambda i: (0,) * array.ndim)
        plane = pl.BlockSpec((1, size_x, size_y), lambda i: (i, 0, 0))
        scalar = pl.BlockSpec(memory_space=pltpu.SMEM)
        packed_shape = (rows_px, rows_py, depth, rows_y, BLOCK)
        packed = pl.BlockSpec((rows_px, rows_py, 1, rows_y, BLOCK), lambda i: (0, 0, i, 0, 0))
        params = pltpu.CompilerParams(vmem_limit_bytes=VMEM_BYTES)

        flops = 2 * 3 * 2 * depth * size_x * size_y * size_x
        sent = pl.pallas_call(
            synthesis_kernel,
            grid=(depth,),
            in_specs=[scalar, plane, plane] + [whole(table) for table in tables],
            out_specs=packed,
            out_shape=jax.ShapeDtypeStruct(packed_shape, jnp.float32),
            compiler_params=params,
            cost_estimate=pl.CostEstimate(flops=flops, bytes_accessed=8 * 2**20, transcendentals=0),
            name="synthesis",
        )(first, white_noise, mode_amplitude, *tables)

        chunk = depth * rows_y
        sent, extra = lax.optimization_barrier((sent, extra))
        field = lax.all_to_all(
            sent.reshape(devices, chunk, BLOCK), ("px", "py"), split_axis=0, concat_axis=0, tiled=True
        )

        held = jnp.concatenate([counts.reshape(-1, BLOCK), extra], axis=0)
        picked = held.at[slot_grid.reshape(-1)].get(mode="promise_in_bounds")
        galaxy = picked.reshape(quarters, -1, BLOCK).transpose(0, 2, 1).reshape(size_z, -1).astype(jnp.float32)

        back = pl.pallas_call(
            shell_kernel,
            out_shape=jax.ShapeDtypeStruct((size_z * rows_y, BLOCK), jnp.float32),
            compiler_params=params,
            cost_estimate=pl.CostEstimate(flops=flops, bytes_accessed=8 * 2**20, transcendentals=size_z * 1024),
            name="shell_gradient",
        )(field.reshape(-1, BLOCK), galaxy, bias_grid, density_grid, *[jnp.asarray(part) for part in z_table])

        returned = lax.all_to_all(
            back.reshape(devices, chunk, BLOCK), ("px", "py"), split_axis=0, concat_axis=0, tiled=True
        )
        step_size = adapted_step(accepted)
        steps = jnp.stack([step_size, jnp.sqrt(2.0 * step_size)])
        out_plane = jax.ShapeDtypeStruct(white_noise.shape, jnp.float32)
        return pl.pallas_call(
            analysis_kernel,
            grid=(depth,),
            in_specs=[scalar, scalar, packed, plane, plane, plane] + [whole(table) for table in tables],
            out_specs=(plane, plane),
            out_shape=(out_plane, out_plane),
            compiler_params=params,
            cost_estimate=pl.CostEstimate(flops=flops, bytes_accessed=12 * 2**20, transcendentals=0),
            name="analysis",
        )(first, steps, returned.reshape(packed_shape), white_noise, mode_amplitude, kick_noise, *tables)

    modes = P(("px", "py"), None, None)
    return jax.shard_map(
        body,
        mesh=mesh,
        in_specs=(modes, modes, modes, P("px", "py", None), P("px", "py", None, None, None), P(), P(), P()),
        out_specs=(modes, modes),
        check_vma=False,
    )
```

```python
import math

import jax
import jax.numpy as jnp
import numpy as np
from jax import lax
from jax.experimental import pallas as pl
from jax.experimental.pallas import tpu as pltpu
from jax.sharding import PartitionSpec as P

BLOCK = 128
HALF = BLOCK // 2
WIDTH = 4
VMEM_BYTES = 56 * 1024 * 1024


def scaled_table(order):
    place = np.arange(order)
    angle = (place[:, None] * place[None, :] % order).astype(np.float64) * (2.0 * math.pi / order)
    table = ((np.cos(angle) + np.sin(angle)) / math.sqrt(order)).astype(np.float32)
    high = table.astype(jnp.bfloat16)
    low = (table - high.astype(np.float32)).astype(jnp.bfloat16)
    return high, low


def split(value):
    high = value.astype(jnp.bfloat16)
    low = (value - high.astype(jnp.float32)).astype(jnp.bfloat16)
    return high, low


def product(left, right, contract=((1,), (0,))):
    left_high, left_low = left
    right_high, right_low = right
    dot = lambda a, b: lax.dot_general(a, b, (contract, ((), ())), preferred_element_type=jnp.float32)
    return dot(left_high, right_high) + (dot(left_high, right_low) + dot(left_low, right_high))


def first_half(shape):
    return lax.broadcasted_iota(jnp.int32, shape, len(shape) - 1) % BLOCK < HALF


def swap_halves(value):
    return pltpu.roll(value, HALF, axis=1)


def live_amplitude(first, amplitude):
    rows = lax.broadcasted_iota(jnp.int32, amplitude.shape, 0)
    cols = lax.broadcasted_iota(jnp.int32, amplitude.shape, 1)
    return jnp.where(rows + cols + first == 0, 0.0, amplitude.astype(jnp.float32))


def synthesis_kernel(first_ref, white_ref, amplitude_ref, high_ref, low_ref, out_ref):
    table = (high_ref[...], low_ref[...])
    weighted = live_amplitude(first_ref[0] + pl.program_id(0), amplitude_ref[0]) * white_ref[0]
    passed = product(table, split(weighted), ((1,), (1,)))
    groups, rows_y = out_ref.shape[1], out_ref.shape[3]
    passed = passed.reshape(groups, 2, rows_y, -1)
    lower, upper = (product(split(passed[:, k].reshape(groups * rows_y, -1)), table) for k in range(2))
    for pair in range(out_ref.shape[0] // 2):
        left = lower[:, pair * BLOCK : (pair + 1) * BLOCK]
        right = swap_halves(upper[:, pair * BLOCK : (pair + 1) * BLOCK])
        mask = first_half(left.shape)
        out_ref[2 * pair, :, 0] = jnp.where(mask, left, right).reshape(groups, -1, BLOCK)
        out_ref[2 * pair + 1, :, 0] = jnp.where(mask, right, left).reshape(groups, -1, BLOCK)


def shell_kernel(
    field_any, galaxy_any, bias_ref, density_ref, high_any, low_any, out_any,
    field_ref, galaxy_ref, high_ref, low_ref, grad_high, grad_low, out_ref, in_sems, galaxy_sems, out_sems,
):
    size_z = high_ref.shape[0]
    rows_y = field_ref.shape[0] // size_z
    pairs, quarters = rows_y // 2, size_z // BLOCK
    loads = [
        pltpu.make_async_copy(source, target, in_sems.at[k])
        for k, (source, target) in enumerate(
            [(high_any, high_ref), (field_any, field_ref), (low_any, low_ref)]
        )
    ]
    spans = [slice(2 * step * BLOCK, 2 * (step + 1) * BLOCK) for step in range(pairs)]
    counts = [
        pltpu.make_async_copy(galaxy_any.at[:, span], galaxy_ref.at[:, span], galaxy_sems.at[step])
        for step, span in enumerate(spans)
    ]
    for copy in loads + counts:
        copy.start()
    for copy in loads:
        copy.wait()
    table = (high_ref[...], low_ref[...])
    for step, span in enumerate(spans):
        field = jnp.concatenate(
            [field_ref[pl.ds(2 * step + k, size_z, stride=rows_y), :] for k in range(2)], axis=1
        )
        contrast = product(table, split(field))
        counts[step].wait()
        for quarter in range(quarters):
            depth = slice(quarter * BLOCK, (quarter + 1) * BLOCK)
            bias = bias_ref[quarter : quarter + 1, span]
            density = density_ref[quarter : quarter + 1, span]
            grad = bias * (galaxy_ref[depth, span] - density * jnp.exp(bias * contrast[depth]))
            grad_high[depth, span], grad_low[depth, span] = split(grad)
    grads = (grad_high[...], grad_low[...])
    stores = []
    for quarter in range(quarters):
        depth = slice(quarter * BLOCK, (quarter + 1) * BLOCK)
        back = product((high_ref[depth, :], low_ref[depth, :]), grads)
        start = quarter * BLOCK * rows_y
        for row in range(rows_y):
            out_ref[pl.ds(start + row, BLOCK, stride=rows_y), :] = back[:, row * BLOCK : (row + 1) * BLOCK]
        part = slice(start, start + BLOCK * rows_y)
        stores.append(pltpu.make_async_copy(out_ref.at[part], out_any.at[part], out_sems.at[quarter]))
        stores[-1].start()
    for copy in stores:
        copy.wait()


def analysis_kernel(
    first_ref, step_ref, field_any, white_any, amplitude_any, kick_any, high_any, low_any, grad_any, next_any,
    field_ref, white_ref, amplitude_ref, kick_ref, high_ref, low_ref, grad_ref, next_ref,
    table_sems, field_sems, mode_sems, out_sems,
):
    depth = white_ref.shape[0]
    tables = [
        pltpu.make_async_copy(high_any, high_ref, table_sems.at[0]),
        pltpu.make_async_copy(low_any, low_ref, table_sems.at[1]),
    ]
    fields = [
        pltpu.make_async_copy(field_any.at[:, :, k], field_ref.at[k], field_sems.at[k]) for k in range(depth)
    ]
    modes = [
        [
            pltpu.make_async_copy(source.at[k], target.at[k], mode_sems.at[k, n])
            for n, (source, target) in enumerate(
                [(white_any, white_ref), (amplitude_any, amplitude_ref), (kick_any, kick_ref)]
            )
        ]
        for k in range(depth)
    ]
    for copy in [fields[0], *tables, *fields[1:]] + sum(modes, []):
        copy.start()
    for copy in tables:
        copy.wait()
    table = (high_ref[...], low_ref[...])
    stores = []
    for k in range(depth):
        fields[k].wait()
        lower, upper = [], []
        for pair in range(field_ref.shape[1] // 2):
            left = field_ref[k, 2 * pair].reshape(-1, BLOCK)
            right = field_ref[k, 2 * pair + 1].reshape(-1, BLOCK)
            mask = first_half(left.shape)
            lower.append(jnp.where(mask, left, right))
            upper.append(swap_halves(jnp.where(mask, right, left)))
        groups, rows_y = field_ref.shape[2:4]
        halves = [
            product(split(jnp.concatenate(half, axis=1)), table).reshape(groups, rows_y, -1)
            for half in (lower, upper)
        ]
        passed = jnp.stack(halves, axis=1).reshape(2 * groups * rows_y, -1)
        back = product(split(passed), table, ((0,), (0,)))
        for copy in modes[k]:
            copy.wait()
        white = white_ref[k]
        gradient = live_amplitude(first_ref[0] + k, amplitude_ref[k]) * back - white
        grad_ref[k] = gradient
        next_ref[k] = white + step_ref[0] * gradient + step_ref[1] * kick_ref[k].astype(jnp.float32)
        for n, (source, target) in enumerate([(grad_ref, grad_any), (next_ref, next_any)]):
            stores.append(pltpu.make_async_copy(source.at[k], target.at[k], out_sems.at[k, n]))
            stores[-1].start()
    for copy in stores:
        copy.wait()


def adapted_step(accepted):
    powers = jnp.power(
        jnp.float32(0.9), jnp.arange(accepted.shape[0], dtype=jnp.int32).astype(jnp.float32)
    )
    accept_rate = jnp.float32(0.1) * jnp.sum(accepted.astype(jnp.float32) * powers)
    return jnp.float32(0.02) * jnp.exp(jnp.float32(2.0) * (accept_rate - jnp.float32(0.574)))


def heavy_ranks(counts, keep, heavy, col_index):
    size, capacity, block = counts.shape
    height = size // WIDTH
    parts = counts.reshape(height, WIDTH, capacity, block)
    at_z, at_x = col_index // WIDTH, col_index % WIDTH
    heavy_z, heavy_x = heavy // WIDTH, heavy % WIDTH

    def pick(array, axis, index):
        return lax.dynamic_index_in_dim(array, index, axis, keepdims=False)

    def column(index):
        part = lax.dynamic_slice(parts, (0, index, keep, 0), (height, 1, capacity - keep, block))
        return part.reshape(height, capacity - keep, block)

    mine = column(at_x)
    for shift in range(1, WIDTH):
        pairs = [(i, i // WIDTH * WIDTH + (i + shift) % WIDTH) for i in range(size)]
        arrived = lax.ppermute(column((at_x + shift) % WIDTH), "py", pairs)
        mine = jnp.where((at_x - heavy_x) % WIDTH == shift, arrived, mine)
    bit = 1
    while bit < height:
        mine = mine.reshape(height // (2 * bit), 2, *mine.shape[1:])
        here = at_z // bit % 2
        pairs = [(i, i ^ (bit * WIDTH)) for i in range(size)]
        arrived = lax.ppermute(pick(mine, 1, 1 - here), "py", pairs)
        mine = jnp.where(here == heavy_z // bit % 2, pick(mine, 1, here), arrived)
        bit *= 2
    return mine.reshape(capacity - keep, block)


def solution(mesh):
    rows_px, rows_py = mesh.shape["px"], mesh.shape["py"]
    devices = rows_px * rows_py

    def body(
        white_noise, mode_amplitude, kick_noise, shell_owner, galaxy_counts, shell_bias, shell_density, accepted
    ):
        depth, size_x, size_y = white_noise.shape
        size_z = depth * devices
        span_x, span_y = size_x // rows_px, size_y // rows_py
        rows_y = span_y // 2
        quarters = size_z // BLOCK
        row_index = lax.axis_index("px")
        col_index = lax.axis_index("py")
        first = ((row_index * rows_py + col_index) * depth).reshape(1)

        tables = [jnp.asarray(part) for part in scaled_table(size_x)]

        galaxy_in = galaxy_counts[0, 0]
        blocks, capacity = shell_owner.shape[-1], galaxy_counts.shape[3]
        keep = -(-(-(-(blocks - capacity) // (rows_py - 1))) // 8) * 8
        owner_list = shell_owner.reshape(-1)
        peers = jnp.arange(rows_py, dtype=jnp.int32)
        onehot = owner_list[:, None] == peers[None, :]
        onehot_int = onehot.astype(jnp.int32)
        rank_index = jnp.sum(jnp.cumsum(onehot_int, axis=0) * onehot_int, axis=1) - 1
        heavy = jnp.argmax(jnp.sum(onehot_int, axis=0)).astype(jnp.int32)
        slot_index = jnp.where(
            rank_index < keep, owner_list * keep + rank_index, rows_py * keep + rank_index - keep
        )
        counts = lax.all_to_all(galaxy_in[:, :keep], "py", split_axis=0, concat_axis=0, tiled=True)
        extra = heavy_ranks(galaxy_in, keep, heavy, col_index)
        bias_row = lax.dynamic_index_in_dim(shell_bias, row_index, 0, keepdims=False)
        density_row = lax.dynamic_index_in_dim(shell_density, row_index, 0, keepdims=False)

        def by_column(blocks):
            grid = blocks.reshape(span_x, 2, rows_y, quarters)
            grid = jnp.where(row_index % 2 == 0, grid, grid[:, ::-1])
            return grid.transpose(3, 2, 1, 0).reshape(quarters, -1)

        slot_grid = by_column(slot_index)
        owner_grid = by_column(owner_list)
        hit = owner_grid[:, :, None] == peers
        bias_grid = jnp.sum(jnp.where(hit, bias_row, 0.0), axis=-1)
        density_grid = jnp.sum(jnp.where(hit, density_row, 0.0), axis=-1)

        whole = lambda array: pl.BlockSpec(array.shape, lambda i: (0,) * array.ndim)
        plane = pl.BlockSpec((1, size_x, size_y), lambda i: (i, 0, 0))
        scalar = pl.BlockSpec(memory_space=pltpu.SMEM)
        packed_shape = (rows_px, rows_py, depth, rows_y, BLOCK)
        packed = pl.BlockSpec((rows_px, rows_py, 1, rows_y, BLOCK), lambda i: (0, 0, i, 0, 0))
        params = pltpu.CompilerParams(vmem_limit_bytes=VMEM_BYTES)

        flops = 2 * 3 * 2 * depth * size_x * size_y * size_x
        sent = pl.pallas_call(
            synthesis_kernel,
            grid=(depth,),
            in_specs=[scalar, plane, plane] + [whole(table) for table in tables],
            out_specs=packed,
            out_shape=jax.ShapeDtypeStruct(packed_shape, jnp.float32),
            compiler_params=params,
            cost_estimate=pl.CostEstimate(flops=flops, bytes_accessed=8 * 2**20, transcendentals=0),
            name="synthesis",
        )(first, white_noise, mode_amplitude, *tables)

        chunk = depth * rows_y
        field = lax.all_to_all(
            sent.reshape(devices, chunk, BLOCK), ("px", "py"), split_axis=0, concat_axis=0, tiled=True
        )

        held = jnp.concatenate([counts.reshape(-1, BLOCK), extra], axis=0)
        picked = held.at[slot_grid.reshape(-1)].get(mode="promise_in_bounds")
        galaxy = picked.reshape(quarters, -1, BLOCK).transpose(0, 2, 1).reshape(size_z, -1).astype(jnp.float32)

        anywhere = pl.BlockSpec(memory_space=pl.ANY)
        inside = pl.BlockSpec(memory_space=pltpu.VMEM)
        table_shapes = [pltpu.VMEM(table.shape, jnp.bfloat16) for table in tables]
        cells = (size_z * rows_y, BLOCK)
        back = pl.pallas_call(
            shell_kernel,
            in_specs=[anywhere, anywhere, inside, inside, anywhere, anywhere],
            out_specs=anywhere,
            out_shape=jax.ShapeDtypeStruct(cells, jnp.float32),
            scratch_shapes=[
                pltpu.VMEM(cells, jnp.float32),
                pltpu.VMEM(galaxy.shape, jnp.float32),
                *table_shapes,
                pltpu.VMEM(galaxy.shape, jnp.bfloat16),
                pltpu.VMEM(galaxy.shape, jnp.bfloat16),
                pltpu.VMEM(cells, jnp.float32),
                pltpu.SemaphoreType.DMA((3,)),
                pltpu.SemaphoreType.DMA((rows_y // 2,)),
                pltpu.SemaphoreType.DMA((quarters,)),
            ],
            compiler_params=params,
            cost_estimate=pl.CostEstimate(flops=flops, bytes_accessed=8 * 2**20, transcendentals=size_z * 1024),
            name="shell_gradient",
        )(field.reshape(cells), galaxy, bias_grid, density_grid, *tables)

        returned = lax.all_to_all(
            back.reshape(devices, chunk, BLOCK), ("px", "py"), split_axis=0, concat_axis=0, tiled=True
        )
        step_size = adapted_step(accepted)
        steps = jnp.stack([step_size, jnp.sqrt(2.0 * step_size)])
        out_plane = jax.ShapeDtypeStruct(white_noise.shape, jnp.float32)
        return pl.pallas_call(
            analysis_kernel,
            in_specs=[scalar, scalar] + [anywhere] * 6,
            out_specs=(anywhere, anywhere),
            out_shape=(out_plane, out_plane),
            scratch_shapes=[
                pltpu.VMEM((depth, rows_px, rows_py, rows_y, BLOCK), jnp.float32),
                pltpu.VMEM(white_noise.shape, jnp.float32),
                pltpu.VMEM(white_noise.shape, jnp.bfloat16),
                pltpu.VMEM(white_noise.shape, jnp.bfloat16),
                *table_shapes,
                pltpu.VMEM(white_noise.shape, jnp.float32),
                pltpu.VMEM(white_noise.shape, jnp.float32),
                pltpu.SemaphoreType.DMA((2,)),
                pltpu.SemaphoreType.DMA((depth,)),
                pltpu.SemaphoreType.DMA((depth, 3)),
                pltpu.SemaphoreType.DMA((depth, 2)),
            ],
            compiler_params=params,
            cost_estimate=pl.CostEstimate(flops=flops, bytes_accessed=12 * 2**20, transcendentals=0),
            name="analysis",
        )(first, steps, returned.reshape(packed_shape), white_noise, mode_amplitude, kick_noise, *tables)

    modes = P(("px", "py"), None, None)
    return jax.shard_map(
        body,
        mesh=mesh,
        in_specs=(modes, modes, modes, P("px", "py", None), P("px", "py", None, None, None), P(), P(), P()),
        out_specs=(modes, modes),
        check_vma=False,
    )
```

```python
import math

import jax
import jax.numpy as jnp
import numpy as np
from jax import lax
from jax.experimental import pallas as pl
from jax.experimental.pallas import tpu as pltpu
from jax.sharding import PartitionSpec as P

BLOCK = 128
HALF = BLOCK // 2
WIDTH = 4
VMEM_BYTES = 56 * 1024 * 1024


def half_tables(order):
    place = np.arange(order // 2)
    parts = []
    for rows in (2 * place, 2 * place + 1):
        angle = (rows[:, None] * place[None, :] % order).astype(np.float64) * (2.0 * math.pi / order)
        parts.append(((np.cos(angle) + np.sin(angle)) / math.sqrt(order)).astype(np.float32))
    parts.append(parts[1].T)
    pairs = []
    for part in parts:
        high = part.astype(jnp.bfloat16)
        pairs += [high, (part - high.astype(np.float32)).astype(jnp.bfloat16)]
    return np.stack(pairs)


def split(value):
    high = value.astype(jnp.bfloat16)
    low = (value - high.astype(jnp.float32)).astype(jnp.bfloat16)
    return high, low


def product(left, right, contract=((1,), (0,))):
    left_high, left_low = left
    right_high, right_low = right
    dot = lambda a, b: lax.dot_general(a, b, (contract, ((), ())), preferred_element_type=jnp.float32)
    return dot(left_high, right_high) + (dot(left_high, right_low) + dot(left_low, right_high))


def first_half(shape):
    return lax.broadcasted_iota(jnp.int32, shape, len(shape) - 1) % BLOCK < HALF


def swap_halves(value):
    return pltpu.roll(value, HALF, axis=1)


def live_amplitude(first, amplitude):
    rows = lax.broadcasted_iota(jnp.int32, amplitude.shape, 0)
    cols = lax.broadcasted_iota(jnp.int32, amplitude.shape, 1)
    return jnp.where(rows + cols + first == 0, 0.0, amplitude.astype(jnp.float32))


def table_pairs(tables_ref):
    return [(tables_ref[2 * n], tables_ref[2 * n + 1]) for n in range(3)]


def fold(value, axis):
    left, right = jnp.split(value, 2, axis=axis)
    return left + right, left - right


def unfold(even, odd, axis):
    return jnp.concatenate([even + odd, even - odd], axis=axis)


def synthesis_kernel(first_ref, white_ref, amplitude_ref, tables_ref, out_ref, weighted_ref):
    even_table, odd_table, _ = table_pairs(tables_ref)
    tiles, size, _ = weighted_ref.shape
    weighted = live_amplitude(first_ref[0] + pl.program_id(0), amplitude_ref[0]) * white_ref[0]
    for tile in range(tiles):
        weighted_ref[tile] = weighted[:, tile * BLOCK : (tile + 1) * BLOCK]
    transposed = ((1,), (1,))
    passed = []
    for parity in range(2):
        rows = [weighted_ref[tile, pl.ds(parity, size // 2, stride=2), :] for tile in range(tiles)]
        total, change = fold(jnp.concatenate(rows, axis=1), 1)
        passed.append(
            (product(even_table, split(total), transposed), product(odd_table, split(change), transposed))
        )
    lower, upper = (
        unfold(product(split(passed[0][k]), even_table), product(split(passed[1][k]), odd_table), 1)
        for k in range(2)
    )
    groups = out_ref.shape[1]
    for pair in range(out_ref.shape[0] // 2):
        left = lower[:, pair * BLOCK : (pair + 1) * BLOCK]
        right = swap_halves(upper[:, pair * BLOCK : (pair + 1) * BLOCK])
        mask = first_half(left.shape)
        out_ref[2 * pair, :, 0] = jnp.where(mask, left, right).reshape(groups, -1, BLOCK)
        out_ref[2 * pair + 1, :, 0] = jnp.where(mask, right, left).reshape(groups, -1, BLOCK)


def shell_kernel(field_ref, galaxy_ref, bias_ref, density_ref, tables_ref, out_ref):
    even_table, odd_table, odd_transposed = table_pairs(tables_ref)
    half_z = tables_ref.shape[1]
    rows_y = field_ref.shape[0] // (2 * half_z)
    for step in range(rows_y // 2):
        fields = [
            jnp.concatenate(
                [
                    field_ref[pl.ds(parity * rows_y + 2 * step + k, half_z, stride=2 * rows_y), :]
                    for k in range(2)
                ],
                axis=1,
            )
            for parity in range(2)
        ]
        contrast = unfold(product(even_table, split(fields[0])), product(odd_transposed, split(fields[1])), 0)
        span = slice(2 * step * BLOCK, 2 * (step + 1) * BLOCK)
        grads = []
        for quarter in range(2 * half_z // BLOCK):
            depth = slice(quarter * BLOCK, (quarter + 1) * BLOCK)
            bias = bias_ref[quarter : quarter + 1, span]
            density = density_ref[quarter : quarter + 1, span]
            grads.append(bias * (galaxy_ref[depth, span] - density * jnp.exp(bias * contrast[depth])))
        total, change = fold(jnp.concatenate(grads, axis=0), 0)
        for parity, back in enumerate([product(even_table, split(total)), product(odd_table, split(change))]):
            for k in range(2):
                row = pl.ds(parity * rows_y + 2 * step + k, half_z, stride=2 * rows_y)
                out_ref[row, :] = back[:, k * BLOCK : (k + 1) * BLOCK]


def analysis_kernel(
    first_ref, step_ref, field_ref, white_ref, amplitude_ref, kick_ref, tables_ref, grad_ref, next_ref, back_ref
):
    even_table, odd_table, _ = table_pairs(tables_ref)
    tiles, size, _ = back_ref.shape
    lower, upper = [], []
    for pair in range(field_ref.shape[0] // 2):
        left = field_ref[2 * pair, :, 0].reshape(-1, BLOCK)
        right = field_ref[2 * pair + 1, :, 0].reshape(-1, BLOCK)
        mask = first_half(left.shape)
        lower.append(jnp.where(mask, left, right))
        upper.append(swap_halves(jnp.where(mask, right, left)))
    transposed = ((1,), (1,))
    folded = [fold(jnp.concatenate(part, axis=1), 1) for part in (lower, upper)]
    for parity, table in enumerate([even_table, odd_table]):
        passed = [split(product(table, split(part[parity]), transposed)) for part in folded]
        back = unfold(product(passed[0], even_table), product(passed[1], odd_table), 1)
        for tile in range(tiles):
            rows = pl.ds(parity, size // 2, stride=2)
            back_ref[tile, rows, :] = back[:, tile * BLOCK : (tile + 1) * BLOCK]
    back = jnp.concatenate([back_ref[tile] for tile in range(tiles)], axis=1)
    white = white_ref[0]
    gradient = live_amplitude(first_ref[0] + pl.program_id(0), amplitude_ref[0]) * back - white
    grad_ref[0] = gradient
    next_ref[0] = white + step_ref[0] * gradient + step_ref[1] * kick_ref[0].astype(jnp.float32)


def adapted_step(accepted):
    powers = jnp.power(
        jnp.float32(0.9), jnp.arange(accepted.shape[0], dtype=jnp.int32).astype(jnp.float32)
    )
    accept_rate = jnp.float32(0.1) * jnp.sum(accepted.astype(jnp.float32) * powers)
    return jnp.float32(0.02) * jnp.exp(jnp.float32(2.0) * (accept_rate - jnp.float32(0.574)))


def heavy_ranks(counts, keep, heavy, col_index, sent):
    size, capacity, block = counts.shape
    height = size // WIDTH
    parts = counts.reshape(height, WIDTH, capacity, block)
    at_z, at_x = col_index // WIDTH, col_index % WIDTH
    heavy_z, heavy_x = heavy // WIDTH, heavy % WIDTH

    def pick(array, axis, index):
        return lax.dynamic_index_in_dim(array, index, axis, keepdims=False)

    def column(index):
        part = lax.dynamic_slice(parts, (0, index, keep, 0), (height, 1, capacity - keep, block))
        return part.reshape(height, capacity - keep, block)

    mine = column(at_x)
    for shift in range(1, WIDTH):
        pairs = [(i, i // WIDTH * WIDTH + (i + shift) % WIDTH) for i in range(size)]
        arrived = lax.ppermute(column((at_x + shift) % WIDTH), "py", pairs)
        mine = jnp.where((at_x - heavy_x) % WIDTH == shift, arrived, mine)
    mine, sent = lax.optimization_barrier((mine, sent))
    low = 4
    mine = mine.reshape(height // low, low, capacity - keep, block)
    here = at_z % low
    away = here ^ (heavy_z % low)
    best = pick(mine, 1, here)
    for flip in range(1, low):
        pairs = [(i, i ^ (flip * WIDTH)) for i in range(size)]
        arrived = lax.ppermute(pick(mine, 1, here ^ flip), "py", pairs)
        best = jnp.where(away == flip, arrived, best)
    here = at_z // low
    away = (here - heavy_z // low) % (height // low)
    mine = pick(best, 0, here)
    for shift in range(1, height // low):
        pairs = [(i, (i + shift * low * WIDTH) % size) for i in range(size)]
        arrived = lax.ppermute(pick(best, 0, (here + shift) % (height // low)), "py", pairs)
        mine = jnp.where(away == shift, arrived, mine)
    return lax.optimization_barrier((mine, sent))


def solution(mesh):
    rows_px, rows_py = mesh.shape["px"], mesh.shape["py"]
    devices = rows_px * rows_py

    def body(
        white_noise, mode_amplitude, kick_noise, shell_owner, galaxy_counts, shell_bias, shell_density, accepted
    ):
        depth, size_x, size_y = white_noise.shape
        size_z = depth * devices
        span_x, span_y = size_x // rows_px, size_y // rows_py
        rows_y = span_y // 2
        quarters = size_z // BLOCK
        row_index = lax.axis_index("px")
        col_index = lax.axis_index("py")
        first = ((row_index * rows_py + col_index) * depth).reshape(1)

        tables = jnp.asarray(half_tables(size_x))

        galaxy_in = galaxy_counts[0, 0]
        blocks, capacity = shell_owner.shape[-1], galaxy_counts.shape[3]
        keep = -(-(-(-(blocks - capacity) // (rows_py - 1))) // 8) * 8
        owner_list = shell_owner.reshape(-1)
        peers = jnp.arange(rows_py, dtype=jnp.int32)
        onehot = owner_list[:, None] == peers[None, :]
        onehot_int = onehot.astype(jnp.int32)
        rank_index = jnp.sum(jnp.cumsum(onehot_int, axis=0) * onehot_int, axis=1) - 1
        heavy = jnp.argmax(jnp.sum(onehot_int, axis=0)).astype(jnp.int32)
        slot_index = jnp.where(
            rank_index < keep, owner_list * keep + rank_index, rows_py * keep + rank_index - keep
        )
        counts = lax.all_to_all(galaxy_in[:, :keep], "py", split_axis=0, concat_axis=0, tiled=True)
        bias_row = lax.dynamic_index_in_dim(shell_bias, row_index, 0, keepdims=False)
        density_row = lax.dynamic_index_in_dim(shell_density, row_index, 0, keepdims=False)

        def by_column(blocks):
            grid = blocks.reshape(span_x, rows_y, 2, quarters)
            grid = jnp.where(row_index % 2 == 0, grid, grid[:, :, ::-1])
            return grid.transpose(3, 1, 2, 0).reshape(quarters, -1)

        slot_grid = by_column(slot_index)
        owner_grid = by_column(owner_list)
        hit = owner_grid[:, :, None] == peers
        bias_grid = jnp.sum(jnp.where(hit, bias_row, 0.0), axis=-1)
        density_grid = jnp.sum(jnp.where(hit, density_row, 0.0), axis=-1)

        whole = lambda array: pl.BlockSpec(array.shape, lambda i: (0,) * array.ndim)
        plane = pl.BlockSpec((1, size_x, size_y), lambda i: (i, 0, 0))
        scalar = pl.BlockSpec(memory_space=pltpu.SMEM)
        packed_shape = (rows_px, rows_py, depth, rows_y, BLOCK)
        packed = pl.BlockSpec((rows_px, rows_py, 1, rows_y, BLOCK), lambda i: (0, 0, i, 0, 0))
        tiled = pltpu.VMEM((size_y // BLOCK, size_x, BLOCK), jnp.float32)
        params = pltpu.CompilerParams(vmem_limit_bytes=VMEM_BYTES)

        flops = 3 * 2 * depth * size_x * size_y * size_x
        sent = pl.pallas_call(
            synthesis_kernel,
            grid=(depth,),
            in_specs=[scalar, plane, plane, whole(tables)],
            out_specs=packed,
            scratch_shapes=[tiled],
            out_shape=jax.ShapeDtypeStruct(packed_shape, jnp.float32),
            compiler_params=params,
            cost_estimate=pl.CostEstimate(flops=flops, bytes_accessed=8 * 2**20, transcendentals=0),
            name="synthesis",
        )(first, white_noise, mode_amplitude, tables)

        chunk = depth * rows_y
        extra, sent = heavy_ranks(galaxy_in, keep, heavy, col_index, sent)
        field = lax.all_to_all(
            sent.reshape(devices, chunk, BLOCK), ("px", "py"), split_axis=0, concat_axis=0, tiled=True
        )

        held = jnp.concatenate([counts.reshape(-1, BLOCK), extra], axis=0)
        picked = held.at[slot_grid.reshape(-1)].get(mode="promise_in_bounds")
        galaxy = picked.reshape(quarters, -1, BLOCK).transpose(0, 2, 1).reshape(size_z, -1).astype(jnp.float32)

        cells = (size_z * rows_y, BLOCK)
        back = pl.pallas_call(
            shell_kernel,
            out_shape=jax.ShapeDtypeStruct(cells, jnp.float32),
            compiler_params=params,
            cost_estimate=pl.CostEstimate(flops=flops, bytes_accessed=8 * 2**20, transcendentals=size_z * 1024),
            name="shell_gradient",
        )(field.reshape(cells), galaxy, bias_grid, density_grid, tables)

        returned = lax.all_to_all(
            back.reshape(devices, chunk, BLOCK), ("px", "py"), split_axis=0, concat_axis=0, tiled=True
        )
        step_size = adapted_step(accepted)
        steps = jnp.stack([step_size, jnp.sqrt(2.0 * step_size)])
        out_plane = jax.ShapeDtypeStruct(white_noise.shape, jnp.float32)
        return pl.pallas_call(
            analysis_kernel,
            grid=(depth,),
            in_specs=[scalar, scalar, packed, plane, plane, plane, whole(tables)],
            out_specs=(plane, plane),
            out_shape=(out_plane, out_plane),
            scratch_shapes=[tiled],
            compiler_params=params,
            cost_estimate=pl.CostEstimate(flops=flops, bytes_accessed=12 * 2**20, transcendentals=0),
            name="analysis",
        )(first, steps, returned.reshape(packed_shape), white_noise, mode_amplitude, kick_noise, tables)

    modes = P(("px", "py"), None, None)
    return jax.shard_map(
        body,
        mesh=mesh,
        in_specs=(modes, modes, modes, P("px", "py", None), P("px", "py", None, None, None), P(), P(), P()),
        out_specs=(modes, modes),
        check_vma=False,
    )
```

```python
import math

import jax
import jax.numpy as jnp
import numpy as np
from jax import lax
from jax.experimental import pallas as pl
from jax.experimental.pallas import tpu as pltpu
from jax.sharding import PartitionSpec as P

BLOCK = 128
HALF = BLOCK // 2
WIDTH = 4
GROUP = 64
VMEM_BYTES = 56 * 1024 * 1024


def half_tables(order):
    place = np.arange(order // 2)
    parts = []
    for rows in (2 * place, 2 * place + 1):
        angle = (rows[:, None] * place[None, :] % order).astype(np.float64) * (2.0 * math.pi / order)
        parts.append(((np.cos(angle) + np.sin(angle)) / math.sqrt(order)).astype(np.float32))
    parts.append(parts[1].T)
    pairs = []
    for part in parts:
        high = part.astype(jnp.bfloat16)
        pairs += [high, (part - high.astype(np.float32)).astype(jnp.bfloat16)]
    return np.stack(pairs)


def split(value):
    high = value.astype(jnp.bfloat16)
    low = (value - high.astype(jnp.float32)).astype(jnp.bfloat16)
    return high, low


def product(left, right, contract=((1,), (0,))):
    left_high, left_low = left
    right_high, right_low = right
    dot = lambda a, b: lax.dot_general(a, b, (contract, ((), ())), preferred_element_type=jnp.float32)
    return dot(left_high, right_high) + (dot(left_high, right_low) + dot(left_low, right_high))


def first_half(shape):
    return lax.broadcasted_iota(jnp.int32, shape, len(shape) - 1) % BLOCK < HALF


def swap_halves(value):
    return pltpu.roll(value, HALF, axis=1)


def live_amplitude(first, amplitude):
    rows = lax.broadcasted_iota(jnp.int32, amplitude.shape, 0)
    cols = lax.broadcasted_iota(jnp.int32, amplitude.shape, 1)
    return jnp.where(rows + cols + first == 0, 0.0, amplitude.astype(jnp.float32))


def table_pairs(tables_ref):
    return [(tables_ref[2 * n], tables_ref[2 * n + 1]) for n in range(3)]


def fold(value, axis):
    left, right = jnp.split(value, 2, axis=axis)
    return left + right, left - right


def unfold(even, odd, axis):
    return jnp.concatenate([even + odd, even - odd], axis=axis)


def synthesis_kernel(first_ref, white_ref, amplitude_ref, tables_ref, out_ref, weighted_ref):
    even_table, odd_table, _ = table_pairs(tables_ref)
    tiles, size, _ = weighted_ref.shape
    weighted = live_amplitude(first_ref[0] + pl.program_id(0), amplitude_ref[0]) * white_ref[0]
    for tile in range(tiles):
        weighted_ref[tile] = weighted[:, tile * BLOCK : (tile + 1) * BLOCK]
    transposed = ((1,), (1,))
    passed = []
    for parity in range(2):
        rows = [weighted_ref[tile, pl.ds(parity, size // 2, stride=2), :] for tile in range(tiles)]
        total, change = fold(jnp.concatenate(rows, axis=1), 1)
        passed.append(
            (product(even_table, split(total), transposed), product(odd_table, split(change), transposed))
        )
    lower, upper = (
        unfold(product(split(passed[0][k]), even_table), product(split(passed[1][k]), odd_table), 1)
        for k in range(2)
    )
    groups = out_ref.shape[1]
    for pair in range(out_ref.shape[0] // 2):
        left = lower[:, pair * BLOCK : (pair + 1) * BLOCK]
        right = swap_halves(upper[:, pair * BLOCK : (pair + 1) * BLOCK])
        mask = first_half(left.shape)
        out_ref[2 * pair, :, 0] = jnp.where(mask, left, right).reshape(groups, -1, BLOCK)
        out_ref[2 * pair + 1, :, 0] = jnp.where(mask, right, left).reshape(groups, -1, BLOCK)


def expected_kernel(field_ref, bias_ref, density_ref, tables_ref, out_ref):
    even_table, _, odd_transposed = table_pairs(tables_ref)
    half_z = tables_ref.shape[1]
    rows_y = field_ref.shape[0] // (2 * half_z)
    for step in range(rows_y // 2):
        fields = [
            jnp.concatenate(
                [
                    field_ref[pl.ds(parity * rows_y + 2 * step + k, half_z, stride=2 * rows_y), :]
                    for k in range(2)
                ],
                axis=1,
            )
            for parity in range(2)
        ]
        contrast = unfold(product(even_table, split(fields[0])), product(odd_transposed, split(fields[1])), 0)
        span = slice(2 * step * BLOCK, 2 * (step + 1) * BLOCK)
        for quarter in range(2 * half_z // BLOCK):
            depth = slice(quarter * BLOCK, (quarter + 1) * BLOCK)
            bias = bias_ref[quarter : quarter + 1, span]
            density = density_ref[quarter : quarter + 1, span]
            out_ref[depth, span] = bias * (density * jnp.exp(bias * contrast[depth]))


def gradient_kernel(
    slot_ref, counts_ref, bias_ref, expected_any, tables_ref, out_ref, rows_ref, expected_ref, sem
):
    load = pltpu.make_async_copy(expected_any, expected_ref, sem)
    load.start()

    def gather(group, carry):
        base = pl.multiple_of(group * GROUP, GROUP)
        for k in range(GROUP):
            rows_ref[pl.ds(base + k, 1), :] = counts_ref[pl.ds(slot_ref[base + k], 1), :]
        return carry

    lax.fori_loop(0, rows_ref.shape[0] // GROUP, gather, 0)
    load.wait()
    even_table, odd_table, _ = table_pairs(tables_ref)
    half_z = tables_ref.shape[1]
    rows_y = out_ref.shape[0] // (2 * half_z)
    columns = expected_ref.shape[1]
    for step in range(rows_y // 2):
        span = slice(2 * step * BLOCK, 2 * (step + 1) * BLOCK)
        grads = []
        for quarter in range(2 * half_z // BLOCK):
            depth = slice(quarter * BLOCK, (quarter + 1) * BLOCK)
            starts = [quarter * columns + (2 * step + k) * BLOCK for k in range(2)]
            galaxy = jnp.concatenate(
                [rows_ref[start : start + BLOCK, :].astype(jnp.float32).T for start in starts], axis=1
            )
            grads.append(bias_ref[quarter : quarter + 1, span] * galaxy - expected_ref[depth, span])
        total, change = fold(jnp.concatenate(grads, axis=0), 0)
        for parity, back in enumerate([product(even_table, split(total)), product(odd_table, split(change))]):
            for k in range(2):
                row = pl.ds(parity * rows_y + 2 * step + k, half_z, stride=2 * rows_y)
                out_ref[row, :] = back[:, k * BLOCK : (k + 1) * BLOCK]


def analysis_kernel(
    first_ref, step_ref, field_ref, white_ref, amplitude_ref, kick_ref, tables_ref, grad_ref, next_ref, back_ref
):
    even_table, odd_table, _ = table_pairs(tables_ref)
    tiles, size, _ = back_ref.shape
    lower, upper = [], []
    for pair in range(field_ref.shape[0] // 2):
        left = field_ref[2 * pair, :, 0].reshape(-1, BLOCK)
        right = field_ref[2 * pair + 1, :, 0].reshape(-1, BLOCK)
        mask = first_half(left.shape)
        lower.append(jnp.where(mask, left, right))
        upper.append(swap_halves(jnp.where(mask, right, left)))
    transposed = ((1,), (1,))
    folded = [fold(jnp.concatenate(part, axis=1), 1) for part in (lower, upper)]
    for parity, table in enumerate([even_table, odd_table]):
        passed = [split(product(table, split(part[parity]), transposed)) for part in folded]
        back = unfold(product(passed[0], even_table), product(passed[1], odd_table), 1)
        for tile in range(tiles):
            rows = pl.ds(parity, size // 2, stride=2)
            back_ref[tile, rows, :] = back[:, tile * BLOCK : (tile + 1) * BLOCK]
    back = jnp.concatenate([back_ref[tile] for tile in range(tiles)], axis=1)
    white = white_ref[0]
    gradient = live_amplitude(first_ref[0] + pl.program_id(0), amplitude_ref[0]) * back - white
    grad_ref[0] = gradient
    next_ref[0] = white + step_ref[0] * gradient + step_ref[1] * kick_ref[0].astype(jnp.float32)


def adapted_step(accepted):
    powers = jnp.power(
        jnp.float32(0.9), jnp.arange(accepted.shape[0], dtype=jnp.int32).astype(jnp.float32)
    )
    accept_rate = jnp.float32(0.1) * jnp.sum(accepted.astype(jnp.float32) * powers)
    return jnp.float32(0.02) * jnp.exp(jnp.float32(2.0) * (accept_rate - jnp.float32(0.574)))


def spread_ranks(counts, keep, heavy, col_index):
    size, capacity, _ = counts.shape
    width = (capacity - keep) // WIDTH
    away = (col_index - heavy) % WIDTH
    part = lambda k: counts[:, keep + k * width : keep + (k + 1) * width]
    mine = part(0)
    for shift in range(1, WIDTH):
        pairs = [(i, i // WIDTH * WIDTH + (i + shift) % WIDTH) for i in range(size)]
        mine = jnp.where(away == shift, lax.ppermute(part(shift), "py", pairs), mine)
    return mine


def solution(mesh):
    rows_px, rows_py = mesh.shape["px"], mesh.shape["py"]
    devices = rows_px * rows_py

    def body(
        white_noise, mode_amplitude, kick_noise, shell_owner, galaxy_counts, shell_bias, shell_density, accepted
    ):
        depth, size_x, size_y = white_noise.shape
        size_z = depth * devices
        span_x, span_y = size_x // rows_px, size_y // rows_py
        rows_y = span_y // 2
        quarters = size_z // BLOCK
        row_index = lax.axis_index("px")
        col_index = lax.axis_index("py")
        first = ((row_index * rows_py + col_index) * depth).reshape(1)

        tables = jnp.asarray(half_tables(size_x))

        galaxy_in = galaxy_counts[0, 0]
        blocks, capacity = shell_owner.shape[-1], galaxy_counts.shape[3]
        keep = -(-(-(-(blocks - capacity) // (rows_py - 1))) // 8) * 8
        owner_list = shell_owner.reshape(-1)
        peers = jnp.arange(rows_py, dtype=jnp.int32)
        onehot = owner_list[:, None] == peers[None, :]
        onehot_int = onehot.astype(jnp.int32)
        rank_index = jnp.sum(jnp.cumsum(onehot_int, axis=0) * onehot_int, axis=1) - 1
        heavy = jnp.argmax(jnp.sum(onehot_int, axis=0)).astype(jnp.int32)
        width = (capacity - keep) // WIDTH
        place = rank_index - keep
        holder = owner_list // WIDTH * WIDTH + (owner_list + place // width) % WIDTH
        slot_index = jnp.where(
            place < 0,
            owner_list * (keep + width) + rank_index,
            holder * (keep + width) + keep + place % width,
        )
        bias_row = lax.dynamic_index_in_dim(shell_bias, row_index, 0, keepdims=False)
        density_row = lax.dynamic_index_in_dim(shell_density, row_index, 0, keepdims=False)

        def by_column(blocks):
            grid = blocks.reshape(span_x, rows_y, 2, quarters)
            grid = jnp.where(row_index % 2 == 0, grid, grid[:, :, ::-1])
            return grid.transpose(3, 1, 2, 0).reshape(quarters, -1)

        slot_grid = by_column(slot_index)
        owner_grid = by_column(owner_list)
        hit = owner_grid[:, :, None] == peers
        bias_grid = jnp.sum(jnp.where(hit, bias_row, 0.0), axis=-1)
        density_grid = jnp.sum(jnp.where(hit, density_row, 0.0), axis=-1)

        whole = lambda array: pl.BlockSpec(array.shape, lambda i: (0,) * array.ndim)
        plane = pl.BlockSpec((1, size_x, size_y), lambda i: (i, 0, 0))
        scalar = pl.BlockSpec(memory_space=pltpu.SMEM)
        packed_shape = (rows_px, rows_py, depth, rows_y, BLOCK)
        packed = pl.BlockSpec((rows_px, rows_py, 1, rows_y, BLOCK), lambda i: (0, 0, i, 0, 0))
        tiled = pltpu.VMEM((size_y // BLOCK, size_x, BLOCK), jnp.float32)
        params = pltpu.CompilerParams(vmem_limit_bytes=VMEM_BYTES)

        flops = 3 * 2 * depth * size_x * size_y * size_x
        sent = pl.pallas_call(
            synthesis_kernel,
            grid=(depth,),
            in_specs=[scalar, plane, plane, whole(tables)],
            out_specs=packed,
            scratch_shapes=[tiled],
            out_shape=jax.ShapeDtypeStruct(packed_shape, jnp.float32),
            compiler_params=params,
            cost_estimate=pl.CostEstimate(flops=flops, bytes_accessed=8 * 2**20, transcendentals=0),
            name="synthesis",
        )(first, white_noise, mode_amplitude, tables)

        chunk = depth * rows_y
        field = lax.all_to_all(
            sent.reshape(devices, chunk, BLOCK), ("px", "py"), split_axis=0, concat_axis=0, tiled=True
        )

        outgoing = jnp.concatenate([galaxy_in[:, :keep], spread_ranks(galaxy_in, keep, heavy, col_index)], axis=1)
        outgoing, field = lax.optimization_barrier((outgoing, field))
        counts = lax.all_to_all(outgoing, "py", split_axis=0, concat_axis=0, tiled=True)

        cells = (size_z * rows_y, BLOCK)
        columns = span_x * span_y
        expected = pl.pallas_call(
            expected_kernel,
            out_shape=jax.ShapeDtypeStruct((size_z, columns), jnp.float32),
            compiler_params=params,
            cost_estimate=pl.CostEstimate(
                flops=flops // 2, bytes_accessed=4 * 2**20, transcendentals=size_z * columns
            ),
            name="expected_counts",
        )(field.reshape(cells), bias_grid, density_grid, tables)
        inside = pl.BlockSpec(memory_space=pltpu.VMEM)
        back = pl.pallas_call(
            gradient_kernel,
            in_specs=[scalar, inside, inside, pl.BlockSpec(memory_space=pl.ANY), inside],
            out_shape=jax.ShapeDtypeStruct(cells, jnp.float32),
            scratch_shapes=[
                pltpu.VMEM((quarters * columns, BLOCK), counts.dtype),
                pltpu.VMEM(expected.shape, jnp.float32),
                pltpu.SemaphoreType.DMA,
            ],
            compiler_params=params,
            cost_estimate=pl.CostEstimate(flops=flops // 2, bytes_accessed=8 * 2**20, transcendentals=0),
            name="shell_gradient",
        )(slot_grid.reshape(-1), counts.reshape(-1, BLOCK), bias_grid, expected, tables)

        returned = lax.all_to_all(
            back.reshape(devices, chunk, BLOCK), ("px", "py"), split_axis=0, concat_axis=0, tiled=True
        )
        step_size = adapted_step(accepted)
        steps = jnp.stack([step_size, jnp.sqrt(2.0 * step_size)])
        out_plane = jax.ShapeDtypeStruct(white_noise.shape, jnp.float32)
        return pl.pallas_call(
            analysis_kernel,
            grid=(depth,),
            in_specs=[scalar, scalar, packed, plane, plane, plane, whole(tables)],
            out_specs=(plane, plane),
            out_shape=(out_plane, out_plane),
            scratch_shapes=[tiled],
            compiler_params=params,
            cost_estimate=pl.CostEstimate(flops=flops, bytes_accessed=12 * 2**20, transcendentals=0),
            name="analysis",
        )(first, steps, returned.reshape(packed_shape), white_noise, mode_amplitude, kick_noise, tables)

    modes = P(("px", "py"), None, None)
    return jax.shard_map(
        body,
        mesh=mesh,
        in_specs=(modes, modes, modes, P("px", "py", None), P("px", "py", None, None, None), P(), P(), P()),
        out_specs=(modes, modes),
        check_vma=False,
    )
```

```python
import math

import jax
import jax.numpy as jnp
import numpy as np
from jax import lax
from jax.experimental import pallas as pl
from jax.experimental.pallas import tpu as pltpu
from jax.sharding import PartitionSpec as P

BLOCK = 128
HALF = BLOCK // 2
WIDTH = 4
GROUP = 128
VMEM_BYTES = 56 * 1024 * 1024


def half_tables(order):
    place = np.arange(order // 2)
    parts = []
    for rows in (2 * place, 2 * place + 1):
        angle = (rows[:, None] * place[None, :] % order).astype(np.float64) * (2.0 * math.pi / order)
        parts.append(((np.cos(angle) + np.sin(angle)) / math.sqrt(order)).astype(np.float32))
    parts.append(parts[1].T)
    pairs = []
    for part in parts:
        high = part.astype(jnp.bfloat16)
        pairs += [high, (part - high.astype(np.float32)).astype(jnp.bfloat16)]
    return np.stack(pairs)


def split(value):
    high = value.astype(jnp.bfloat16)
    low = (value - high.astype(jnp.float32)).astype(jnp.bfloat16)
    return high, low


def product(left, right, contract=((1,), (0,))):
    left_high, left_low = left
    right_high, right_low = right
    dot = lambda a, b: lax.dot_general(a, b, (contract, ((), ())), preferred_element_type=jnp.float32)
    return dot(left_high, right_high) + (dot(left_high, right_low) + dot(left_low, right_high))


def first_half(shape):
    return lax.broadcasted_iota(jnp.int32, shape, len(shape) - 1) % BLOCK < HALF


def swap_halves(value):
    return pltpu.roll(value, HALF, axis=1)


def live_amplitude(first, amplitude):
    rows = lax.broadcasted_iota(jnp.int32, amplitude.shape, 0)
    cols = lax.broadcasted_iota(jnp.int32, amplitude.shape, 1)
    return jnp.where(rows + cols + first == 0, 0.0, amplitude.astype(jnp.float32))


def table_pairs(tables_ref):
    return [(tables_ref[2 * n], tables_ref[2 * n + 1]) for n in range(3)]


def fold(value, axis):
    left, right = jnp.split(value, 2, axis=axis)
    return left + right, left - right


def unfold(even, odd, axis):
    return jnp.concatenate([even + odd, even - odd], axis=axis)


def synthesis_kernel(first_ref, white_ref, amplitude_ref, tables_ref, out_ref, weighted_ref):
    even_table, odd_table, _ = table_pairs(tables_ref)
    tiles, size, _ = weighted_ref.shape
    weighted = live_amplitude(first_ref[0] + pl.program_id(0), amplitude_ref[0]) * white_ref[0]
    for tile in range(tiles):
        weighted_ref[tile] = weighted[:, tile * BLOCK : (tile + 1) * BLOCK]
    transposed = ((1,), (1,))
    passed = []
    for parity in range(2):
        rows = [weighted_ref[tile, pl.ds(parity, size // 2, stride=2), :] for tile in range(tiles)]
        total, change = fold(jnp.concatenate(rows, axis=1), 1)
        passed.append(
            (product(even_table, split(total), transposed), product(odd_table, split(change), transposed))
        )
    lower, upper = (
        unfold(product(split(passed[0][k]), even_table), product(split(passed[1][k]), odd_table), 1)
        for k in range(2)
    )
    groups = out_ref.shape[1]
    for pair in range(out_ref.shape[0] // 2):
        left = lower[:, pair * BLOCK : (pair + 1) * BLOCK]
        right = swap_halves(upper[:, pair * BLOCK : (pair + 1) * BLOCK])
        mask = first_half(left.shape)
        out_ref[2 * pair, :, 0] = jnp.where(mask, left, right).reshape(groups, -1, BLOCK)
        out_ref[2 * pair + 1, :, 0] = jnp.where(mask, right, left).reshape(groups, -1, BLOCK)


def expected_kernel(field_ref, bias_ref, density_ref, tables_ref, out_ref):
    even_table, _, odd_transposed = table_pairs(tables_ref)
    half_z = tables_ref.shape[1]
    rows_y = field_ref.shape[0] // (2 * half_z)
    for step in range(rows_y // 2):
        fields = [
            jnp.concatenate(
                [
                    field_ref[pl.ds(parity * rows_y + 2 * step + k, half_z, stride=2 * rows_y), :]
                    for k in range(2)
                ],
                axis=1,
            )
            for parity in range(2)
        ]
        contrast = unfold(product(even_table, split(fields[0])), product(odd_transposed, split(fields[1])), 0)
        span = slice(2 * step * BLOCK, 2 * (step + 1) * BLOCK)
        for quarter in range(2 * half_z // BLOCK):
            depth = slice(quarter * BLOCK, (quarter + 1) * BLOCK)
            bias = bias_ref[quarter : quarter + 1, span]
            density = density_ref[quarter : quarter + 1, span]
            out_ref[depth, span] = bias * (density * jnp.exp(bias * contrast[depth]))


def gradient_kernel(
    slot_ref, counts_ref, bias_ref, expected_any, tables_ref, out_ref, rows_ref, expected_ref, sem
):
    load = pltpu.make_async_copy(expected_any, expected_ref, sem)
    load.start()

    def gather(group, carry):
        base = pl.multiple_of(group * GROUP, GROUP)
        for k in range(GROUP):
            rows_ref[pl.ds(base + k, 1), :] = counts_ref[pl.ds(slot_ref[base + k], 1), :]
        return carry

    lax.fori_loop(0, rows_ref.shape[0] // GROUP, gather, 0)
    load.wait()
    even_table, odd_table, _ = table_pairs(tables_ref)
    half_z = tables_ref.shape[1]
    rows_y = out_ref.shape[0] // (2 * half_z)
    columns = expected_ref.shape[1]
    for step in range(rows_y // 2):
        span = slice(2 * step * BLOCK, 2 * (step + 1) * BLOCK)
        grads = []
        for quarter in range(2 * half_z // BLOCK):
            depth = slice(quarter * BLOCK, (quarter + 1) * BLOCK)
            starts = [quarter * columns + (2 * step + k) * BLOCK for k in range(2)]
            galaxy = jnp.concatenate(
                [rows_ref[start : start + BLOCK, :].astype(jnp.float32).T for start in starts], axis=1
            )
            grads.append(bias_ref[quarter : quarter + 1, span] * galaxy - expected_ref[depth, span])
        total, change = fold(jnp.concatenate(grads, axis=0), 0)
        for parity, back in enumerate([product(even_table, split(total)), product(odd_table, split(change))]):
            for k in range(2):
                row = pl.ds(parity * rows_y + 2 * step + k, half_z, stride=2 * rows_y)
                out_ref[row, :] = back[:, k * BLOCK : (k + 1) * BLOCK]


def analysis_kernel(
    first_ref, step_ref, field_ref, white_ref, amplitude_ref, kick_ref, tables_ref, grad_ref, next_ref, back_ref
):
    even_table, odd_table, _ = table_pairs(tables_ref)
    tiles, size, _ = back_ref.shape
    lower, upper = [], []
    for pair in range(field_ref.shape[0] // 2):
        left = field_ref[2 * pair, :, 0].reshape(-1, BLOCK)
        right = field_ref[2 * pair + 1, :, 0].reshape(-1, BLOCK)
        mask = first_half(left.shape)
        lower.append(jnp.where(mask, left, right))
        upper.append(swap_halves(jnp.where(mask, right, left)))
    transposed = ((1,), (1,))
    folded = [fold(jnp.concatenate(part, axis=1), 1) for part in (lower, upper)]
    for parity, table in enumerate([even_table, odd_table]):
        passed = [split(product(table, split(part[parity]), transposed)) for part in folded]
        back = unfold(product(passed[0], even_table), product(passed[1], odd_table), 1)
        for tile in range(tiles):
            rows = pl.ds(parity, size // 2, stride=2)
            back_ref[tile, rows, :] = back[:, tile * BLOCK : (tile + 1) * BLOCK]
    back = jnp.concatenate([back_ref[tile] for tile in range(tiles)], axis=1)
    white = white_ref[0]
    gradient = live_amplitude(first_ref[0] + pl.program_id(0), amplitude_ref[0]) * back - white
    grad_ref[0] = gradient
    next_ref[0] = white + step_ref[0] * gradient + step_ref[1] * kick_ref[0].astype(jnp.float32)


def adapted_step(accepted):
    powers = jnp.power(
        jnp.float32(0.9), jnp.arange(accepted.shape[0], dtype=jnp.int32).astype(jnp.float32)
    )
    accept_rate = jnp.float32(0.1) * jnp.sum(accepted.astype(jnp.float32) * powers)
    return jnp.float32(0.02) * jnp.exp(jnp.float32(2.0) * (accept_rate - jnp.float32(0.574)))


def spread_ranks(counts, keep, heavy, col_index):
    size, capacity, _ = counts.shape
    width = (capacity - keep) // WIDTH
    away = (col_index - heavy) % WIDTH
    part = lambda k: counts[:, keep + k * width : keep + (k + 1) * width]
    mine = part(0)
    for shift in range(1, WIDTH):
        pairs = [(i, i // WIDTH * WIDTH + (i + shift) % WIDTH) for i in range(size)]
        mine = jnp.where(away == shift, lax.ppermute(part(shift), "py", pairs), mine)
    return mine


def solution(mesh):
    rows_px, rows_py = mesh.shape["px"], mesh.shape["py"]
    devices = rows_px * rows_py

    def body(
        white_noise, mode_amplitude, kick_noise, shell_owner, galaxy_counts, shell_bias, shell_density, accepted
    ):
        depth, size_x, size_y = white_noise.shape
        size_z = depth * devices
        span_x, span_y = size_x // rows_px, size_y // rows_py
        rows_y = span_y // 2
        quarters = size_z // BLOCK
        row_index = lax.axis_index("px")
        col_index = lax.axis_index("py")
        first = ((row_index * rows_py + col_index) * depth).reshape(1)

        tables = jnp.asarray(half_tables(size_x))

        galaxy_in = galaxy_counts[0, 0]
        blocks, capacity = shell_owner.shape[-1], galaxy_counts.shape[3]
        keep = -(-(-(-(blocks - capacity) // (rows_py - 1))) // 8) * 8
        owner_list = shell_owner.reshape(-1)
        peers = jnp.arange(rows_py, dtype=jnp.int32)
        onehot = owner_list[:, None] == peers[None, :]
        onehot_int = onehot.astype(jnp.int32)
        rank_index = jnp.sum(jnp.cumsum(onehot_int, axis=0) * onehot_int, axis=1) - 1
        heavy = jnp.argmax(jnp.sum(onehot_int, axis=0)).astype(jnp.int32)
        width = (capacity - keep) // WIDTH
        place = rank_index - keep
        holder = owner_list // WIDTH * WIDTH + (owner_list + place // width) % WIDTH
        slot_index = jnp.where(
            place < 0,
            owner_list * (keep + width) + rank_index,
            holder * (keep + width) + keep + place % width,
        )
        bias_row = lax.dynamic_index_in_dim(shell_bias, row_index, 0, keepdims=False)
        density_row = lax.dynamic_index_in_dim(shell_density, row_index, 0, keepdims=False)

        def by_column(blocks):
            grid = blocks.reshape(span_x, rows_y, 2, quarters)
            grid = jnp.where(row_index % 2 == 0, grid, grid[:, :, ::-1])
            return grid.transpose(3, 1, 2, 0).reshape(quarters, -1)

        slot_grid = by_column(slot_index)
        owner_grid = by_column(owner_list)
        hit = owner_grid[:, :, None] == peers
        bias_grid = jnp.sum(jnp.where(hit, bias_row, 0.0), axis=-1)
        density_grid = jnp.sum(jnp.where(hit, density_row, 0.0), axis=-1)

        whole = lambda array: pl.BlockSpec(array.shape, lambda i: (0,) * array.ndim)
        plane = pl.BlockSpec((1, size_x, size_y), lambda i: (i, 0, 0))
        scalar = pl.BlockSpec(memory_space=pltpu.SMEM)
        packed_shape = (rows_px, rows_py, depth, rows_y, BLOCK)
        packed = pl.BlockSpec((rows_px, rows_py, 1, rows_y, BLOCK), lambda i: (0, 0, i, 0, 0))
        tiled = pltpu.VMEM((size_y // BLOCK, size_x, BLOCK), jnp.float32)
        params = pltpu.CompilerParams(vmem_limit_bytes=VMEM_BYTES)

        flops = 3 * 2 * depth * size_x * size_y * size_x
        sent = pl.pallas_call(
            synthesis_kernel,
            grid=(depth,),
            in_specs=[scalar, plane, plane, whole(tables)],
            out_specs=packed,
            scratch_shapes=[tiled],
            out_shape=jax.ShapeDtypeStruct(packed_shape, jnp.float32),
            compiler_params=params,
            cost_estimate=pl.CostEstimate(flops=flops, bytes_accessed=8 * 2**20, transcendentals=0),
            name="synthesis",
        )(first, white_noise, mode_amplitude, tables)

        chunk = depth * rows_y
        field = lax.all_to_all(
            sent.reshape(devices, chunk, BLOCK), ("px", "py"), split_axis=0, concat_axis=0, tiled=True
        )

        outgoing = jnp.concatenate([galaxy_in[:, :keep], spread_ranks(galaxy_in, keep, heavy, col_index)], axis=1)
        outgoing, field = lax.optimization_barrier((outgoing, field))
        counts = lax.all_to_all(outgoing, "py", split_axis=0, concat_axis=0, tiled=True)

        cells = (size_z * rows_y, BLOCK)
        columns = span_x * span_y
        expected = pl.pallas_call(
            expected_kernel,
            out_shape=jax.ShapeDtypeStruct((size_z, columns), jnp.float32),
            compiler_params=pltpu.CompilerParams(vmem_limit_bytes=48 * 2**20),
            cost_estimate=pl.CostEstimate(
                flops=flops // 2, bytes_accessed=4 * 2**20, transcendentals=size_z * columns
            ),
            name="expected_counts",
        )(field.reshape(cells), bias_grid, density_grid, tables)
        inside = pl.BlockSpec(memory_space=pltpu.VMEM)
        back = pl.pallas_call(
            gradient_kernel,
            in_specs=[scalar, inside, inside, pl.BlockSpec(memory_space=pl.ANY), inside],
            out_shape=jax.ShapeDtypeStruct(cells, jnp.float32),
            scratch_shapes=[
                pltpu.VMEM((quarters * columns, BLOCK), counts.dtype),
                pltpu.VMEM(expected.shape, jnp.float32),
                pltpu.SemaphoreType.DMA,
            ],
            compiler_params=pltpu.CompilerParams(vmem_limit_bytes=56 * 2**20),
            cost_estimate=pl.CostEstimate(flops=flops // 2, bytes_accessed=8 * 2**20, transcendentals=0),
            name="shell_gradient",
        )(slot_grid.reshape(-1), counts.reshape(-1, BLOCK), bias_grid, expected, tables)

        returned = lax.all_to_all(
            back.reshape(devices, chunk, BLOCK), ("px", "py"), split_axis=0, concat_axis=0, tiled=True
        )
        step_size = adapted_step(accepted)
        steps = jnp.stack([step_size, jnp.sqrt(2.0 * step_size)])
        out_plane = jax.ShapeDtypeStruct(white_noise.shape, jnp.float32)
        return pl.pallas_call(
            analysis_kernel,
            grid=(depth,),
            in_specs=[scalar, scalar, packed, plane, plane, plane, whole(tables)],
            out_specs=(plane, plane),
            out_shape=(out_plane, out_plane),
            scratch_shapes=[tiled],
            compiler_params=pltpu.CompilerParams(vmem_limit_bytes=50 * 2**20),
            cost_estimate=pl.CostEstimate(flops=flops, bytes_accessed=12 * 2**20, transcendentals=0),
            name="analysis",
        )(first, steps, returned.reshape(packed_shape), white_noise, mode_amplitude, kick_noise, tables)

    modes = P(("px", "py"), None, None)
    return jax.shard_map(
        body,
        mesh=mesh,
        in_specs=(modes, modes, modes, P("px", "py", None), P("px", "py", None, None, None), P(), P(), P()),
        out_specs=(modes, modes),
        check_vma=False,
    )
```

```python
import math

import jax
import jax.numpy as jnp
import numpy as np
from jax import lax
from jax.experimental import pallas as pl
from jax.experimental.pallas import tpu as pltpu
from jax.sharding import PartitionSpec as P

BLOCK = 128
HALF = BLOCK // 2
WIDTH = 4
GROUP = 128
VMEM_BYTES = 56 * 1024 * 1024


def half_tables(order):
    place = np.arange(order // 2)
    parts = []
    for rows in (2 * place, 2 * place + 1):
        angle = (rows[:, None] * place[None, :] % order).astype(np.float64) * (2.0 * math.pi / order)
        parts.append(((np.cos(angle) + np.sin(angle)) / math.sqrt(order)).astype(np.float32))
    parts.append(parts[1].T)
    pairs = []
    for part in parts:
        high = part.astype(jnp.bfloat16)
        pairs += [high, (part - high.astype(np.float32)).astype(jnp.bfloat16)]
    return np.stack(pairs)


def split(value):
    high = value.astype(jnp.bfloat16)
    low = (value - high.astype(jnp.float32)).astype(jnp.bfloat16)
    return high, low


def product(left, right, contract=((1,), (0,))):
    left_high, left_low = left
    right_high, right_low = right
    dot = lambda a, b: lax.dot_general(a, b, (contract, ((), ())), preferred_element_type=jnp.float32)
    return dot(left_high, right_high) + (dot(left_high, right_low) + dot(left_low, right_high))


def first_half(shape):
    return lax.broadcasted_iota(jnp.int32, shape, len(shape) - 1) % BLOCK < HALF


def swap_halves(value):
    return pltpu.roll(value, HALF, axis=1)


def live_amplitude(first, amplitude):
    rows = lax.broadcasted_iota(jnp.int32, amplitude.shape, 0)
    cols = lax.broadcasted_iota(jnp.int32, amplitude.shape, 1)
    return jnp.where(rows + cols + first == 0, 0.0, amplitude.astype(jnp.float32))


def table_pairs(tables_ref):
    return [(tables_ref[2 * n], tables_ref[2 * n + 1]) for n in range(3)]


def fold(value, axis):
    left, right = jnp.split(value, 2, axis=axis)
    return left + right, left - right


def unfold(even, odd, axis):
    return jnp.concatenate([even + odd, even - odd], axis=axis)


def synthesis_kernel(first_ref, white_ref, amplitude_ref, tables_ref, out_ref, weighted_ref):
    even_table, odd_table, _ = table_pairs(tables_ref)
    tiles, size, _ = weighted_ref.shape
    weighted = live_amplitude(first_ref[0] + pl.program_id(0), amplitude_ref[0]) * white_ref[0]
    for tile in range(tiles):
        weighted_ref[tile] = weighted[:, tile * BLOCK : (tile + 1) * BLOCK]
    transposed = ((1,), (1,))
    passed = []
    for parity in range(2):
        rows = [weighted_ref[tile, pl.ds(parity, size // 2, stride=2), :] for tile in range(tiles)]
        total, change = fold(jnp.concatenate(rows, axis=1), 1)
        passed.append(
            (product(even_table, split(total), transposed), product(odd_table, split(change), transposed))
        )
    lower, upper = (
        unfold(product(split(passed[0][k]), even_table), product(split(passed[1][k]), odd_table), 1)
        for k in range(2)
    )
    groups = out_ref.shape[1]
    for pair in range(out_ref.shape[0] // 2):
        left = lower[:, pair * BLOCK : (pair + 1) * BLOCK]
        right = swap_halves(upper[:, pair * BLOCK : (pair + 1) * BLOCK])
        mask = first_half(left.shape)
        out_ref[2 * pair, :, 0] = jnp.where(mask, left, right).reshape(groups, -1, BLOCK)
        out_ref[2 * pair + 1, :, 0] = jnp.where(mask, right, left).reshape(groups, -1, BLOCK)


def expected_kernel(field_ref, bias_ref, density_ref, tables_ref, out_ref):
    even_table, _, odd_transposed = table_pairs(tables_ref)
    half_z = tables_ref.shape[1]
    rows_y = field_ref.shape[0] // (2 * half_z)
    for step in range(rows_y // 2):
        fields = [
            jnp.concatenate(
                [
                    field_ref[pl.ds(parity * rows_y + 2 * step + k, half_z, stride=2 * rows_y), :]
                    for k in range(2)
                ],
                axis=1,
            )
            for parity in range(2)
        ]
        contrast = unfold(product(even_table, split(fields[0])), product(odd_transposed, split(fields[1])), 0)
        span = slice(2 * step * BLOCK, 2 * (step + 1) * BLOCK)
        for quarter in range(2 * half_z // BLOCK):
            depth = slice(quarter * BLOCK, (quarter + 1) * BLOCK)
            bias = bias_ref[quarter : quarter + 1, span]
            density = density_ref[quarter : quarter + 1, span]
            out_ref[depth, span] = bias * (density * jnp.exp(bias * contrast[depth]))


def gradient_kernel(
    slot_ref, counts_ref, bias_ref, expected_any, tables_ref, out_ref, rows_ref, expected_ref, sem
):
    load = pltpu.make_async_copy(expected_any, expected_ref, sem)
    load.start()

    def gather(group, carry):
        base = pl.multiple_of(group * GROUP, GROUP)
        for k in range(GROUP):
            rows_ref[pl.ds(base + k, 1), :] = counts_ref[pl.ds(slot_ref[base + k], 1), :]
        return carry

    lax.fori_loop(0, rows_ref.shape[0] // GROUP, gather, 0)
    load.wait()
    even_table, odd_table, _ = table_pairs(tables_ref)
    half_z = tables_ref.shape[1]
    rows_y = out_ref.shape[0] // (2 * half_z)
    columns = expected_ref.shape[1]
    for step in range(rows_y // 2):
        span = slice(2 * step * BLOCK, 2 * (step + 1) * BLOCK)
        grads = []
        for quarter in range(2 * half_z // BLOCK):
            depth = slice(quarter * BLOCK, (quarter + 1) * BLOCK)
            starts = [quarter * columns + (2 * step + k) * BLOCK for k in range(2)]
            galaxy = jnp.concatenate(
                [rows_ref[start : start + BLOCK, :].astype(jnp.float32).T for start in starts], axis=1
            )
            grads.append(bias_ref[quarter : quarter + 1, span] * galaxy - expected_ref[depth, span])
        total, change = fold(jnp.concatenate(grads, axis=0), 0)
        for parity, back in enumerate([product(even_table, split(total)), product(odd_table, split(change))]):
            for k in range(2):
                row = pl.ds(parity * rows_y + 2 * step + k, half_z, stride=2 * rows_y)
                out_ref[row, :] = back[:, k * BLOCK : (k + 1) * BLOCK]


def analysis_kernel(
    first_ref, step_ref, field_ref, white_ref, amplitude_ref, kick_ref, tables_ref, grad_ref, next_ref, back_ref
):
    even_table, odd_table, _ = table_pairs(tables_ref)
    tiles, size, _ = back_ref.shape
    lower, upper = [], []
    for pair in range(field_ref.shape[0] // 2):
        left = field_ref[2 * pair, :, 0].reshape(-1, BLOCK)
        right = field_ref[2 * pair + 1, :, 0].reshape(-1, BLOCK)
        mask = first_half(left.shape)
        lower.append(jnp.where(mask, left, right))
        upper.append(swap_halves(jnp.where(mask, right, left)))
    transposed = ((1,), (1,))
    folded = [fold(jnp.concatenate(part, axis=1), 1) for part in (lower, upper)]
    for parity, table in enumerate([even_table, odd_table]):
        passed = [split(product(table, split(part[parity]), transposed)) for part in folded]
        back = unfold(product(passed[0], even_table), product(passed[1], odd_table), 1)
        for tile in range(tiles):
            rows = pl.ds(parity, size // 2, stride=2)
            back_ref[tile, rows, :] = back[:, tile * BLOCK : (tile + 1) * BLOCK]
    back = jnp.concatenate([back_ref[tile] for tile in range(tiles)], axis=1)
    white = white_ref[0]
    gradient = live_amplitude(first_ref[0] + pl.program_id(0), amplitude_ref[0]) * back - white
    grad_ref[0] = gradient
    next_ref[0] = white + step_ref[0] * gradient + step_ref[1] * kick_ref[0].astype(jnp.float32)


def adapted_step(accepted):
    powers = jnp.power(
        jnp.float32(0.9), jnp.arange(accepted.shape[0], dtype=jnp.int32).astype(jnp.float32)
    )
    accept_rate = jnp.float32(0.1) * jnp.sum(accepted.astype(jnp.float32) * powers)
    return jnp.float32(0.02) * jnp.exp(jnp.float32(2.0) * (accept_rate - jnp.float32(0.574)))


def spread_ranks(counts, keep, heavy, col_index):
    size, capacity, _ = counts.shape
    width = (capacity - keep) // WIDTH
    away = (col_index - heavy) % WIDTH
    part = lambda k: counts[::-1, keep + k * width : keep + (k + 1) * width]
    mine = part(0)
    for shift in range(1, WIDTH):
        pairs = [(i, i // WIDTH * WIDTH + (i + shift) % WIDTH) for i in range(size)]
        mine = jnp.where(away == shift, lax.ppermute(part(shift), "py", pairs), mine)
    return mine


def solution(mesh):
    rows_px, rows_py = mesh.shape["px"], mesh.shape["py"]
    devices = rows_px * rows_py

    def body(
        white_noise, mode_amplitude, kick_noise, shell_owner, galaxy_counts, shell_bias, shell_density, accepted
    ):
        depth, size_x, size_y = white_noise.shape
        size_z = depth * devices
        span_x, span_y = size_x // rows_px, size_y // rows_py
        rows_y = span_y // 2
        quarters = size_z // BLOCK
        row_index = lax.axis_index("px")
        col_index = lax.axis_index("py")
        first = ((row_index * rows_py + col_index) * depth).reshape(1)

        tables = jnp.asarray(half_tables(size_x))

        galaxy_in = galaxy_counts[0, 0]
        blocks, capacity = shell_owner.shape[-1], galaxy_counts.shape[3]
        keep = -(-(-(-(blocks - capacity) // (rows_py - 1))) // 8) * 8
        owner_list = shell_owner.reshape(-1)
        peers = jnp.arange(rows_py, dtype=jnp.int32)
        onehot = owner_list[:, None] == peers[None, :]
        onehot_int = onehot.astype(jnp.int32)
        rank_index = jnp.sum(jnp.cumsum(onehot_int, axis=0) * onehot_int, axis=1) - 1
        heavy = jnp.argmax(jnp.sum(onehot_int, axis=0)).astype(jnp.int32)
        width = (capacity - keep) // WIDTH
        place = rank_index - keep
        holder = owner_list // WIDTH * WIDTH + (owner_list + place // width) % WIDTH
        slot_index = jnp.where(
            place < 0,
            (rows_py - 1 - owner_list) * (keep + width) + rank_index,
            (rows_py - 1 - holder) * (keep + width) + keep + place % width,
        )
        bias_row = lax.dynamic_index_in_dim(shell_bias, row_index, 0, keepdims=False)
        density_row = lax.dynamic_index_in_dim(shell_density, row_index, 0, keepdims=False)

        def by_column(blocks):
            grid = blocks.reshape(span_x, rows_y, 2, quarters)
            grid = jnp.where(row_index % 2 == 0, grid, grid[:, :, ::-1])
            return grid.transpose(3, 1, 2, 0).reshape(quarters, -1)

        slot_grid = by_column(slot_index)
        owner_grid = by_column(owner_list)
        hit = owner_grid[:, :, None] == peers
        bias_grid = jnp.sum(jnp.where(hit, bias_row, 0.0), axis=-1)
        density_grid = jnp.sum(jnp.where(hit, density_row, 0.0), axis=-1)

        whole = lambda array: pl.BlockSpec(array.shape, lambda i: (0,) * array.ndim)
        plane = pl.BlockSpec((1, size_x, size_y), lambda i: (i, 0, 0))
        scalar = pl.BlockSpec(memory_space=pltpu.SMEM)
        packed_shape = (rows_px, rows_py, depth, rows_y, BLOCK)
        packed = pl.BlockSpec((rows_px, rows_py, 1, rows_y, BLOCK), lambda i: (0, 0, i, 0, 0))
        tiled = pltpu.VMEM((size_y // BLOCK, size_x, BLOCK), jnp.float32)
        params = pltpu.CompilerParams(vmem_limit_bytes=VMEM_BYTES)

        flops = 3 * 2 * depth * size_x * size_y * size_x
        sent = pl.pallas_call(
            synthesis_kernel,
            grid=(depth,),
            in_specs=[scalar, plane, plane, whole(tables)],
            out_specs=packed,
            scratch_shapes=[tiled],
            out_shape=jax.ShapeDtypeStruct(packed_shape, jnp.float32),
            compiler_params=params,
            cost_estimate=pl.CostEstimate(flops=flops, bytes_accessed=8 * 2**20, transcendentals=0),
            name="synthesis",
        )(first, white_noise, mode_amplitude, tables)

        chunk = depth * rows_y
        field = lax.all_to_all(
            sent.reshape(devices, chunk, BLOCK), ("px", "py"), split_axis=0, concat_axis=0, tiled=True
        )

        outgoing = jnp.concatenate([galaxy_in[::-1, :keep], spread_ranks(galaxy_in, keep, heavy, col_index)], axis=1)
        outgoing, field = lax.optimization_barrier((outgoing, field))
        counts = lax.all_to_all(
            outgoing,
            "py",
            split_axis=0,
            concat_axis=0,
            tiled=True,
            axis_index_groups=[list(range(rows_py - 1, -1, -1))],
        )

        cells = (size_z * rows_y, BLOCK)
        columns = span_x * span_y
        expected = pl.pallas_call(
            expected_kernel,
            out_shape=jax.ShapeDtypeStruct((size_z, columns), jnp.float32),
            compiler_params=pltpu.CompilerParams(vmem_limit_bytes=48 * 2**20),
            cost_estimate=pl.CostEstimate(
                flops=flops // 2, bytes_accessed=4 * 2**20, transcendentals=size_z * columns
            ),
            name="expected_counts",
        )(field.reshape(cells), bias_grid, density_grid, tables)
        inside = pl.BlockSpec(memory_space=pltpu.VMEM)
        back = pl.pallas_call(
            gradient_kernel,
            in_specs=[scalar, inside, inside, pl.BlockSpec(memory_space=pl.ANY), inside],
            out_shape=jax.ShapeDtypeStruct(cells, jnp.float32),
            scratch_shapes=[
                pltpu.VMEM((quarters * columns, BLOCK), counts.dtype),
                pltpu.VMEM(expected.shape, jnp.float32),
                pltpu.SemaphoreType.DMA,
            ],
            compiler_params=pltpu.CompilerParams(vmem_limit_bytes=56 * 2**20),
            cost_estimate=pl.CostEstimate(flops=flops // 2, bytes_accessed=8 * 2**20, transcendentals=0),
            name="shell_gradient",
        )(slot_grid.reshape(-1), counts.reshape(-1, BLOCK), bias_grid, expected, tables)

        returned = lax.all_to_all(
            back.reshape(devices, chunk, BLOCK), ("px", "py"), split_axis=0, concat_axis=0, tiled=True
        )
        step_size = adapted_step(accepted)
        steps = jnp.stack([step_size, jnp.sqrt(2.0 * step_size)])
        out_plane = jax.ShapeDtypeStruct(white_noise.shape, jnp.float32)
        return pl.pallas_call(
            analysis_kernel,
            grid=(depth,),
            in_specs=[scalar, scalar, packed, plane, plane, plane, whole(tables)],
            out_specs=(plane, plane),
            out_shape=(out_plane, out_plane),
            scratch_shapes=[tiled],
            compiler_params=pltpu.CompilerParams(vmem_limit_bytes=50 * 2**20),
            cost_estimate=pl.CostEstimate(flops=flops, bytes_accessed=12 * 2**20, transcendentals=0),
            name="analysis",
        )(first, steps, returned.reshape(packed_shape), white_noise, mode_amplitude, kick_noise, tables)

    modes = P(("px", "py"), None, None)
    return jax.shard_map(
        body,
        mesh=mesh,
        in_specs=(modes, modes, modes, P("px", "py", None), P("px", "py", None, None, None), P(), P(), P()),
        out_specs=(modes, modes),
        check_vma=False,
    )
```

```python
import math

import jax
import jax.numpy as jnp
import numpy as np
from jax import lax
from jax.experimental import pallas as pl
from jax.experimental.pallas import tpu as pltpu
from jax.sharding import PartitionSpec as P

BLOCK = 128
HALF = BLOCK // 2
WIDTH = 4
ROWS = 8
GROUP = 128
VMEM_BYTES = 56 * 1024 * 1024


def half_tables(order):
    place = np.arange(order // 2)
    parts = []
    for rows in (2 * place, 2 * place + 1):
        angle = (rows[:, None] * place[None, :] % order).astype(np.float64) * (2.0 * math.pi / order)
        parts.append(((np.cos(angle) + np.sin(angle)) / math.sqrt(order)).astype(np.float32))
    parts.append(parts[1].T)
    pairs = []
    for part in parts:
        high = part.astype(jnp.bfloat16)
        pairs += [high, (part - high.astype(np.float32)).astype(jnp.bfloat16)]
    return np.stack(pairs)


def split(value):
    high = value.astype(jnp.bfloat16)
    low = (value - high.astype(jnp.float32)).astype(jnp.bfloat16)
    return high, low


def product(left, right, contract=((1,), (0,))):
    left_high, left_low = left
    right_high, right_low = right
    dot = lambda a, b: lax.dot_general(a, b, (contract, ((), ())), preferred_element_type=jnp.float32)
    return dot(left_high, right_high) + (dot(left_high, right_low) + dot(left_low, right_high))


def first_half(shape):
    return lax.broadcasted_iota(jnp.int32, shape, len(shape) - 1) % BLOCK < HALF


def swap_halves(value):
    return pltpu.roll(value, HALF, axis=1)


def live_amplitude(first, amplitude):
    amplitude = amplitude.astype(jnp.float32)
    top = amplitude[:ROWS]
    rows = lax.broadcasted_iota(jnp.int32, top.shape, 0)
    cols = lax.broadcasted_iota(jnp.int32, top.shape, 1)
    top = jnp.where(rows + cols + first == 0, 0.0, top)
    return jnp.concatenate([top, amplitude[ROWS:]], axis=0)


def table_pairs(tables_ref):
    return [(tables_ref[2 * n], tables_ref[2 * n + 1]) for n in range(3)]


def fold(value, axis):
    left, right = jnp.split(value, 2, axis=axis)
    return left + right, left - right


def unfold(even, odd, axis):
    return jnp.concatenate([even + odd, even - odd], axis=axis)


def synthesis_kernel(first_ref, white_ref, amplitude_ref, tables_ref, out_ref, weighted_ref):
    even_table, odd_table, _ = table_pairs(tables_ref)
    tiles, size, _ = weighted_ref.shape
    weighted = live_amplitude(first_ref[0] + pl.program_id(0), amplitude_ref[0]) * white_ref[0]
    for tile in range(tiles):
        weighted_ref[tile] = weighted[:, tile * BLOCK : (tile + 1) * BLOCK]
    transposed = ((1,), (1,))
    passed = []
    for parity in range(2):
        rows = [weighted_ref[tile, pl.ds(parity, size // 2, stride=2), :] for tile in range(tiles)]
        total, change = fold(jnp.concatenate(rows, axis=1), 1)
        passed.append(
            (product(even_table, split(total), transposed), product(odd_table, split(change), transposed))
        )
    lower, upper = (
        unfold(product(split(passed[0][k]), even_table), product(split(passed[1][k]), odd_table), 1)
        for k in range(2)
    )
    groups = out_ref.shape[1]
    for pair in range(out_ref.shape[0] // 2):
        left = lower[:, pair * BLOCK : (pair + 1) * BLOCK]
        right = swap_halves(upper[:, pair * BLOCK : (pair + 1) * BLOCK])
        mask = first_half(left.shape)
        out_ref[2 * pair, :, 0] = jnp.where(mask, left, right).reshape(groups, -1, BLOCK)
        out_ref[2 * pair + 1, :, 0] = jnp.where(mask, right, left).reshape(groups, -1, BLOCK)


def expected_kernel(field_ref, bias_ref, density_ref, tables_ref, out_ref):
    even_table, _, odd_transposed = table_pairs(tables_ref)
    half_z = tables_ref.shape[1]
    rows_y = field_ref.shape[0] // (2 * half_z)
    for step in range(rows_y // 2):
        fields = [
            jnp.concatenate(
                [
                    field_ref[pl.ds(parity * rows_y + 2 * step + k, half_z, stride=2 * rows_y), :]
                    for k in range(2)
                ],
                axis=1,
            )
            for parity in range(2)
        ]
        contrast = unfold(product(even_table, split(fields[0])), product(odd_transposed, split(fields[1])), 0)
        span = slice(2 * step * BLOCK, 2 * (step + 1) * BLOCK)
        for quarter in range(2 * half_z // BLOCK):
            depth = slice(quarter * BLOCK, (quarter + 1) * BLOCK)
            bias = bias_ref[quarter : quarter + 1, span]
            density = density_ref[quarter : quarter + 1, span]
            out_ref[depth, span] = bias * (density * jnp.exp(bias * contrast[depth]))


def gradient_kernel(
    slot_ref, counts_ref, bias_ref, expected_any, tables_ref, out_ref, rows_ref, expected_ref, sem
):
    load = pltpu.make_async_copy(expected_any, expected_ref, sem)
    load.start()

    def gather(group, carry):
        base = pl.multiple_of(group * GROUP, GROUP)
        for k in range(GROUP):
            rows_ref[pl.ds(base + k, 1), :] = counts_ref[pl.ds(slot_ref[base + k], 1), :]
        return carry

    lax.fori_loop(0, rows_ref.shape[0] // GROUP, gather, 0)
    load.wait()
    even_table, odd_table, _ = table_pairs(tables_ref)
    half_z = tables_ref.shape[1]
    rows_y = out_ref.shape[0] // (2 * half_z)
    columns = expected_ref.shape[1]
    for step in range(rows_y // 2):
        span = slice(2 * step * BLOCK, 2 * (step + 1) * BLOCK)
        grads = []
        for quarter in range(2 * half_z // BLOCK):
            depth = slice(quarter * BLOCK, (quarter + 1) * BLOCK)
            starts = [quarter * columns + (2 * step + k) * BLOCK for k in range(2)]
            galaxy = jnp.concatenate(
                [rows_ref[start : start + BLOCK, :].astype(jnp.float32).T for start in starts], axis=1
            )
            grads.append(bias_ref[quarter : quarter + 1, span] * galaxy - expected_ref[depth, span])
        total, change = fold(jnp.concatenate(grads, axis=0), 0)
        for parity, back in enumerate([product(even_table, split(total)), product(odd_table, split(change))]):
            for k in range(2):
                row = pl.ds(parity * rows_y + 2 * step + k, half_z, stride=2 * rows_y)
                out_ref[row, :] = back[:, k * BLOCK : (k + 1) * BLOCK]


def analysis_kernel(
    first_ref, step_ref, field_any, white_any, amplitude_ref, kick_ref, tables_ref,
    grad_any, next_any, field_ref, white_ref, grad_ref, next_ref, back_ref, load_sems, sems,
):
    loads = [
        [
            pltpu.make_async_copy(field_any.at[:, :, plane], field_ref.at[plane], load_sems.at[plane, 0]),
            pltpu.make_async_copy(white_any.at[plane], white_ref.at[plane], load_sems.at[plane, 1]),
        ]
        for plane in range(white_ref.shape[0])
    ]
    for copy in sum(loads, []):
        copy.start()
    even_table, odd_table, _ = table_pairs(tables_ref)
    tiles, size, _ = back_ref.shape
    stores = []
    for plane in range(white_ref.shape[0]):
        loads[plane][0].wait()
        lower, upper = [], []
        for pair in range(field_ref.shape[1] // 2):
            left = field_ref[plane, 2 * pair].reshape(-1, BLOCK)
            right = field_ref[plane, 2 * pair + 1].reshape(-1, BLOCK)
            mask = first_half(left.shape)
            lower.append(jnp.where(mask, left, right))
            upper.append(swap_halves(jnp.where(mask, right, left)))
        transposed = ((1,), (1,))
        folded = [fold(jnp.concatenate(part, axis=1), 1) for part in (lower, upper)]
        for parity, table in enumerate([even_table, odd_table]):
            passed = [split(product(table, split(part[parity]), transposed)) for part in folded]
            back = unfold(product(passed[0], even_table), product(passed[1], odd_table), 1)
            for tile in range(tiles):
                rows = pl.ds(parity, size // 2, stride=2)
                back_ref[tile, rows, :] = back[:, tile * BLOCK : (tile + 1) * BLOCK]
        back = jnp.concatenate([back_ref[tile] for tile in range(tiles)], axis=1)
        loads[plane][1].wait()
        white = white_ref[plane]
        gradient = live_amplitude(first_ref[0] + plane, amplitude_ref[plane]) * back - white
        grad_ref[plane] = gradient
        next_ref[plane] = white + step_ref[0] * gradient + step_ref[1] * kick_ref[plane].astype(jnp.float32)
        for n, (source, target) in enumerate([(grad_ref, grad_any), (next_ref, next_any)]):
            stores.append(pltpu.make_async_copy(source.at[plane], target.at[plane], sems.at[plane, n]))
            stores[-1].start()
    for copy in stores:
        copy.wait()


def adapted_step(accepted):
    powers = jnp.power(
        jnp.float32(0.9), jnp.arange(accepted.shape[0], dtype=jnp.int32).astype(jnp.float32)
    )
    accept_rate = jnp.float32(0.1) * jnp.sum(accepted.astype(jnp.float32) * powers)
    return jnp.float32(0.02) * jnp.exp(jnp.float32(2.0) * (accept_rate - jnp.float32(0.574)))


def spread_ranks(counts, keep, heavy, col_index):
    size, capacity, _ = counts.shape
    width = (capacity - keep) // WIDTH
    away = (col_index - heavy) % WIDTH
    part = lambda k: counts[:, keep + k * width : keep + (k + 1) * width]
    mine = part(0)
    for shift in range(1, WIDTH):
        pairs = [(i, i // WIDTH * WIDTH + (i + shift) % WIDTH) for i in range(size)]
        mine = jnp.where(away == shift, lax.ppermute(part(shift), "py", pairs), mine)
    return mine


def solution(mesh):
    rows_px, rows_py = mesh.shape["px"], mesh.shape["py"]
    devices = rows_px * rows_py

    def body(
        white_noise, mode_amplitude, kick_noise, shell_owner, galaxy_counts, shell_bias, shell_density, accepted
    ):
        depth, size_x, size_y = white_noise.shape
        size_z = depth * devices
        span_x, span_y = size_x // rows_px, size_y // rows_py
        rows_y = span_y // 2
        quarters = size_z // BLOCK
        row_index = lax.axis_index("px")
        col_index = lax.axis_index("py")
        first = ((row_index * rows_py + col_index) * depth).reshape(1)

        tables = jnp.asarray(half_tables(size_x))

        galaxy_in = galaxy_counts[0, 0]
        blocks, capacity = shell_owner.shape[-1], galaxy_counts.shape[3]
        keep = -(-(-(-(blocks - capacity) // (rows_py - 1))) // 8) * 8
        owner_list = shell_owner.reshape(-1)
        peers = jnp.arange(rows_py, dtype=jnp.int32)
        onehot = owner_list[:, None] == peers[None, :]
        onehot_int = onehot.astype(jnp.int32)
        rank_index = jnp.sum(jnp.cumsum(onehot_int, axis=0) * onehot_int, axis=1) - 1
        heavy = jnp.argmax(jnp.sum(onehot_int, axis=0)).astype(jnp.int32)
        width = (capacity - keep) // WIDTH
        place = rank_index - keep
        holder = owner_list // WIDTH * WIDTH + (owner_list + place // width) % WIDTH
        slot_index = jnp.where(
            place < 0,
            owner_list * (keep + width) + rank_index,
            holder * (keep + width) + keep + place % width,
        )
        bias_row = lax.dynamic_index_in_dim(shell_bias, row_index, 0, keepdims=False)
        density_row = lax.dynamic_index_in_dim(shell_density, row_index, 0, keepdims=False)

        def by_column(blocks):
            grid = blocks.reshape(span_x, rows_y, 2, quarters)
            grid = jnp.where(row_index % 2 == 0, grid, grid[:, :, ::-1])
            return grid.transpose(3, 1, 2, 0).reshape(quarters, -1)

        slot_grid = by_column(slot_index)
        owner_grid = by_column(owner_list)
        hit = owner_grid[:, :, None] == peers
        bias_grid = jnp.sum(jnp.where(hit, bias_row, 0.0), axis=-1)
        density_grid = jnp.sum(jnp.where(hit, density_row, 0.0), axis=-1)

        whole = lambda array: pl.BlockSpec(array.shape, lambda i: (0,) * array.ndim)
        plane = pl.BlockSpec((1, size_x, size_y), lambda i: (i, 0, 0))
        scalar = pl.BlockSpec(memory_space=pltpu.SMEM)
        packed_shape = (rows_px, rows_py, depth, rows_y, BLOCK)
        packed = pl.BlockSpec((rows_px, rows_py, 1, rows_y, BLOCK), lambda i: (0, 0, i, 0, 0))
        tiled = pltpu.VMEM((size_y // BLOCK, size_x, BLOCK), jnp.float32)
        params = pltpu.CompilerParams(vmem_limit_bytes=VMEM_BYTES)

        flops = 3 * 2 * depth * size_x * size_y * size_x
        sent = pl.pallas_call(
            synthesis_kernel,
            grid=(depth,),
            in_specs=[scalar, plane, plane, whole(tables)],
            out_specs=packed,
            scratch_shapes=[tiled],
            out_shape=jax.ShapeDtypeStruct(packed_shape, jnp.float32),
            compiler_params=params,
            cost_estimate=pl.CostEstimate(flops=flops, bytes_accessed=8 * 2**20, transcendentals=0),
            name="synthesis",
        )(first, white_noise, mode_amplitude, tables)

        chunk = depth * rows_y
        field = lax.all_to_all(
            sent.reshape(devices, chunk, BLOCK), ("px", "py"), split_axis=0, concat_axis=0, tiled=True
        )

        outgoing = jnp.concatenate([galaxy_in[:, :keep], spread_ranks(galaxy_in, keep, heavy, col_index)], axis=1)
        outgoing, field = lax.optimization_barrier((outgoing, field))
        counts = lax.all_to_all(outgoing, "py", split_axis=0, concat_axis=0, tiled=True)

        cells = (size_z * rows_y, BLOCK)
        columns = span_x * span_y
        expected = pl.pallas_call(
            expected_kernel,
            out_shape=jax.ShapeDtypeStruct((size_z, columns), jnp.float32),
            compiler_params=pltpu.CompilerParams(vmem_limit_bytes=48 * 2**20),
            cost_estimate=pl.CostEstimate(
                flops=flops // 2, bytes_accessed=4 * 2**20, transcendentals=size_z * columns
            ),
            name="expected_counts",
        )(field.reshape(cells), bias_grid, density_grid, tables)
        inside = pl.BlockSpec(memory_space=pltpu.VMEM)
        anywhere = pl.BlockSpec(memory_space=pl.ANY)
        back = pl.pallas_call(
            gradient_kernel,
            in_specs=[scalar, inside, inside, pl.BlockSpec(memory_space=pl.ANY), inside],
            out_shape=jax.ShapeDtypeStruct(cells, jnp.float32),
            scratch_shapes=[
                pltpu.VMEM((quarters * columns, BLOCK), counts.dtype),
                pltpu.VMEM(expected.shape, jnp.float32),
                pltpu.SemaphoreType.DMA,
            ],
            compiler_params=pltpu.CompilerParams(vmem_limit_bytes=56 * 2**20),
            cost_estimate=pl.CostEstimate(flops=flops // 2, bytes_accessed=8 * 2**20, transcendentals=0),
            name="shell_gradient",
        )(slot_grid.reshape(-1), counts.reshape(-1, BLOCK), bias_grid, expected, tables)

        returned = lax.all_to_all(
            back.reshape(devices, chunk, BLOCK), ("px", "py"), split_axis=0, concat_axis=0, tiled=True
        )
        step_size = adapted_step(accepted)
        steps = jnp.stack([step_size, jnp.sqrt(2.0 * step_size)])
        out_plane = jax.ShapeDtypeStruct(white_noise.shape, jnp.float32)
        return pl.pallas_call(
            analysis_kernel,
            in_specs=[scalar, scalar, anywhere, anywhere, inside, inside, inside],
            out_specs=(anywhere, anywhere),
            out_shape=(out_plane, out_plane),
            scratch_shapes=[
                pltpu.VMEM((depth, rows_px, rows_py, rows_y, BLOCK), jnp.float32),
                pltpu.VMEM(white_noise.shape, jnp.float32),
                pltpu.VMEM(white_noise.shape, jnp.float32),
                pltpu.VMEM(white_noise.shape, jnp.float32),
                tiled,
                pltpu.SemaphoreType.DMA((depth, 2)),
                pltpu.SemaphoreType.DMA((depth, 2)),
            ],
            compiler_params=pltpu.CompilerParams(vmem_limit_bytes=50 * 2**20),
            cost_estimate=pl.CostEstimate(flops=flops, bytes_accessed=12 * 2**20, transcendentals=0),
            name="analysis",
        )(first, steps, returned.reshape(packed_shape), white_noise, mode_amplitude, kick_noise, tables)

    modes = P(("px", "py"), None, None)
    return jax.shard_map(
        body,
        mesh=mesh,
        in_specs=(modes, modes, modes, P("px", "py", None), P("px", "py", None, None, None), P(), P(), P()),
        out_specs=(modes, modes),
        check_vma=False,
    )
```

```python
import math

import jax
import jax.numpy as jnp
import numpy as np
from jax import lax
from jax.experimental import pallas as pl
from jax.experimental.pallas import tpu as pltpu
from jax.sharding import PartitionSpec as P

BLOCK = 128
HALF = BLOCK // 2
WIDTH = 4
ROWS = 8
GROUP = 128
VMEM_BYTES = 56 * 1024 * 1024


def half_tables(order):
    place = np.arange(order // 2)
    parts = []
    for rows in (2 * place, 2 * place + 1):
        angle = (rows[:, None] * place[None, :] % order).astype(np.float64) * (2.0 * math.pi / order)
        parts.append(((np.cos(angle) + np.sin(angle)) / math.sqrt(order)).astype(np.float32))
    parts.append(parts[1].T)
    pairs = []
    for part in parts:
        high = part.astype(jnp.bfloat16)
        pairs += [high, (part - high.astype(np.float32)).astype(jnp.bfloat16)]
    return np.stack(pairs)


def split(value):
    high = value.astype(jnp.bfloat16)
    low = (value - high.astype(jnp.float32)).astype(jnp.bfloat16)
    return high, low


def product(left, right, contract=((1,), (0,))):
    left_high, left_low = left
    right_high, right_low = right
    dot = lambda a, b: lax.dot_general(a, b, (contract, ((), ())), preferred_element_type=jnp.float32)
    return dot(left_high, right_high) + (dot(left_high, right_low) + dot(left_low, right_high))


def first_half(shape):
    return lax.broadcasted_iota(jnp.int32, shape, len(shape) - 1) % BLOCK < HALF


def swap_halves(value):
    return pltpu.roll(value, HALF, axis=1)


def live_amplitude(first, amplitude):
    amplitude = amplitude.astype(jnp.float32)
    top = amplitude[:ROWS]
    rows = lax.broadcasted_iota(jnp.int32, top.shape, 0)
    cols = lax.broadcasted_iota(jnp.int32, top.shape, 1)
    top = jnp.where(rows + cols + first == 0, 0.0, top)
    return jnp.concatenate([top, amplitude[ROWS:]], axis=0)


def table_pairs(tables_ref):
    return [(tables_ref[2 * n], tables_ref[2 * n + 1]) for n in range(3)]


def fold(value, axis):
    left, right = jnp.split(value, 2, axis=axis)
    return left + right, left - right


def unfold(even, odd, axis):
    return jnp.concatenate([even + odd, even - odd], axis=axis)


def synthesis_kernel(first_ref, white_ref, amplitude_ref, tables_ref, out_ref, weighted_ref):
    even_table, odd_table, _ = table_pairs(tables_ref)
    tiles, size, _ = weighted_ref.shape
    weighted = live_amplitude(first_ref[0] + pl.program_id(0), amplitude_ref[0]) * white_ref[0]
    for tile in range(tiles):
        weighted_ref[tile] = weighted[:, tile * BLOCK : (tile + 1) * BLOCK]
    transposed = ((1,), (1,))
    passed = []
    for parity in range(2):
        rows = [weighted_ref[tile, pl.ds(parity, size // 2, stride=2), :] for tile in range(tiles)]
        total, change = fold(jnp.concatenate(rows, axis=1), 1)
        passed.append(
            (product(even_table, split(total), transposed), product(odd_table, split(change), transposed))
        )
    lower, upper = (
        unfold(product(split(passed[0][k]), even_table), product(split(passed[1][k]), odd_table), 1)
        for k in range(2)
    )
    groups = out_ref.shape[1]
    for pair in range(out_ref.shape[0] // 2):
        left = lower[:, pair * BLOCK : (pair + 1) * BLOCK]
        right = swap_halves(upper[:, pair * BLOCK : (pair + 1) * BLOCK])
        mask = first_half(left.shape)
        out_ref[2 * pair, :, 0] = jnp.where(mask, left, right).reshape(groups, -1, BLOCK)
        out_ref[2 * pair + 1, :, 0] = jnp.where(mask, right, left).reshape(groups, -1, BLOCK)


def expected_kernel(field_ref, bias_ref, density_ref, tables_ref, out_ref):
    even_table, _, odd_transposed = table_pairs(tables_ref)
    half_z = tables_ref.shape[1]
    rows_y = field_ref.shape[0] // (2 * half_z)
    for step in range(rows_y // 2):
        fields = [
            jnp.concatenate(
                [
                    field_ref[pl.ds(parity * rows_y + 2 * step + k, half_z, stride=2 * rows_y), :]
                    for k in range(2)
                ],
                axis=1,
            )
            for parity in range(2)
        ]
        contrast = unfold(product(even_table, split(fields[0])), product(odd_transposed, split(fields[1])), 0)
        span = slice(2 * step * BLOCK, 2 * (step + 1) * BLOCK)
        for quarter in range(2 * half_z // BLOCK):
            depth = slice(quarter * BLOCK, (quarter + 1) * BLOCK)
            bias = bias_ref[quarter : quarter + 1, span]
            density = density_ref[quarter : quarter + 1, span]
            out_ref[depth, span] = bias * (density * jnp.exp(bias * contrast[depth]))


def gradient_kernel(
    slot_ref, counts_ref, bias_ref, expected_any, tables_ref, out_ref, rows_ref, expected_ref, sem
):
    load = pltpu.make_async_copy(expected_any, expected_ref, sem)
    load.start()

    def gather(group, carry):
        base = pl.multiple_of(group * GROUP, GROUP)
        for k in range(GROUP):
            rows_ref[pl.ds(base + k, 1), :] = counts_ref[pl.ds(slot_ref[base + k], 1), :]
        return carry

    lax.fori_loop(0, rows_ref.shape[0] // GROUP, gather, 0)
    load.wait()
    even_table, odd_table, _ = table_pairs(tables_ref)
    half_z = tables_ref.shape[1]
    rows_y = out_ref.shape[0] // (2 * half_z)
    columns = expected_ref.shape[1]
    for step in range(rows_y // 2):
        span = slice(2 * step * BLOCK, 2 * (step + 1) * BLOCK)
        grads = []
        for quarter in range(2 * half_z // BLOCK):
            depth = slice(quarter * BLOCK, (quarter + 1) * BLOCK)
            starts = [quarter * columns + (2 * step + k) * BLOCK for k in range(2)]
            galaxy = jnp.concatenate(
                [rows_ref[start : start + BLOCK, :].astype(jnp.float32).T for start in starts], axis=1
            )
            grads.append(bias_ref[quarter : quarter + 1, span] * galaxy - expected_ref[depth, span])
        total, change = fold(jnp.concatenate(grads, axis=0), 0)
        for parity, back in enumerate([product(even_table, split(total)), product(odd_table, split(change))]):
            for k in range(2):
                row = pl.ds(parity * rows_y + 2 * step + k, half_z, stride=2 * rows_y)
                out_ref[row, :] = back[:, k * BLOCK : (k + 1) * BLOCK]


def analysis_kernel(
    first_ref, step_ref, field_ref, white_ref, amplitude_ref, kick_ref, tables_ref, grad_ref, next_ref, back_ref
):
    even_table, odd_table, _ = table_pairs(tables_ref)
    tiles, size, _ = back_ref.shape
    lower, upper = [], []
    for pair in range(field_ref.shape[0] // 2):
        left = field_ref[2 * pair, :, 0].reshape(-1, BLOCK)
        right = field_ref[2 * pair + 1, :, 0].reshape(-1, BLOCK)
        mask = first_half(left.shape)
        lower.append(jnp.where(mask, left, right))
        upper.append(swap_halves(jnp.where(mask, right, left)))
    transposed = ((1,), (1,))
    folded = [fold(jnp.concatenate(part, axis=1), 1) for part in (lower, upper)]
    for parity, table in enumerate([even_table, odd_table]):
        passed = [split(product(table, split(part[parity]), transposed)) for part in folded]
        back = unfold(product(passed[0], even_table), product(passed[1], odd_table), 1)
        for tile in range(tiles):
            rows = pl.ds(parity, size // 2, stride=2)
            back_ref[tile, rows, :] = back[:, tile * BLOCK : (tile + 1) * BLOCK]
    back = jnp.concatenate([back_ref[tile] for tile in range(tiles)], axis=1)
    white = white_ref[0]
    gradient = live_amplitude(first_ref[0] + pl.program_id(0), amplitude_ref[0]) * back - white
    grad_ref[0] = gradient
    next_ref[0] = white + step_ref[0] * gradient + step_ref[1] * kick_ref[0].astype(jnp.float32)


def adapted_step(accepted):
    powers = jnp.power(
        jnp.float32(0.9), jnp.arange(accepted.shape[0], dtype=jnp.int32).astype(jnp.float32)
    )
    accept_rate = jnp.float32(0.1) * jnp.sum(accepted.astype(jnp.float32) * powers)
    return jnp.float32(0.02) * jnp.exp(jnp.float32(2.0) * (accept_rate - jnp.float32(0.574)))


def spread_ranks(counts, keep, heavy, col_index):
    size, capacity, _ = counts.shape
    width = (capacity - keep) // WIDTH
    away = (col_index - heavy) % WIDTH
    part = lambda k: counts[:, keep + k * width : keep + (k + 1) * width]
    mine = part(0)
    for shift in range(1, WIDTH):
        pairs = [(i, i // WIDTH * WIDTH + (i + shift) % WIDTH) for i in range(size)]
        mine = jnp.where(away == shift, lax.ppermute(part(shift), "py", pairs), mine)
    return mine


def solution(mesh):
    rows_px, rows_py = mesh.shape["px"], mesh.shape["py"]
    devices = rows_px * rows_py

    def body(
        white_noise, mode_amplitude, kick_noise, shell_owner, galaxy_counts, shell_bias, shell_density, accepted
    ):
        depth, size_x, size_y = white_noise.shape
        size_z = depth * devices
        span_x, span_y = size_x // rows_px, size_y // rows_py
        rows_y = span_y // 2
        quarters = size_z // BLOCK
        row_index = lax.axis_index("px")
        col_index = lax.axis_index("py")
        first = ((row_index * rows_py + col_index) * depth).reshape(1)

        tables = jnp.asarray(half_tables(size_x))

        galaxy_in = galaxy_counts[0, 0]
        blocks, capacity = shell_owner.shape[-1], galaxy_counts.shape[3]
        keep = -(-(-(-(blocks - capacity) // (rows_py - 1))) // 8) * 8
        owner_list = shell_owner.reshape(-1)
        peers = jnp.arange(rows_py, dtype=jnp.int32)
        onehot = owner_list[:, None] == peers[None, :]
        onehot_int = onehot.astype(jnp.int32)
        rank_index = jnp.sum(jnp.cumsum(onehot_int, axis=0) * onehot_int, axis=1) - 1
        heavy = jnp.argmax(jnp.sum(onehot_int, axis=0)).astype(jnp.int32)
        width = (capacity - keep) // WIDTH
        place = rank_index - keep
        holder = owner_list // WIDTH * WIDTH + (owner_list + place // width) % WIDTH
        slot_index = jnp.where(
            place < 0,
            (rows_py - 1 - owner_list) * (keep + width) + rank_index,
            (rows_py - 1 - holder) * (keep + width) + keep + place % width,
        )
        bias_row = lax.dynamic_index_in_dim(shell_bias, row_index, 0, keepdims=False)
        density_row = lax.dynamic_index_in_dim(shell_density, row_index, 0, keepdims=False)

        def by_column(blocks):
            grid = blocks.reshape(span_x, rows_y, 2, quarters)
            grid = jnp.where(row_index % 2 == 0, grid, grid[:, :, ::-1])
            return grid.transpose(3, 1, 2, 0).reshape(quarters, -1)

        slot_grid = by_column(slot_index)
        owner_grid = by_column(owner_list)
        hit = owner_grid[:, :, None] == peers
        bias_grid = jnp.sum(jnp.where(hit, bias_row, 0.0), axis=-1)
        density_grid = jnp.sum(jnp.where(hit, density_row, 0.0), axis=-1)

        whole = lambda array: pl.BlockSpec(array.shape, lambda i: (0,) * array.ndim)
        plane = pl.BlockSpec((1, size_x, size_y), lambda i: (i, 0, 0))
        scalar = pl.BlockSpec(memory_space=pltpu.SMEM)
        packed_shape = (rows_px, rows_py, depth, rows_y, BLOCK)
        packed = pl.BlockSpec((rows_px, rows_py, 1, rows_y, BLOCK), lambda i: (0, 0, i, 0, 0))
        tiled = pltpu.VMEM((size_y // BLOCK, size_x, BLOCK), jnp.float32)
        params = pltpu.CompilerParams(vmem_limit_bytes=VMEM_BYTES)

        flops = 3 * 2 * depth * size_x * size_y * size_x
        sent = pl.pallas_call(
            synthesis_kernel,
            grid=(depth,),
            in_specs=[scalar, plane, plane, whole(tables)],
            out_specs=packed,
            scratch_shapes=[tiled],
            out_shape=jax.ShapeDtypeStruct(packed_shape, jnp.float32),
            compiler_params=params,
            cost_estimate=pl.CostEstimate(flops=flops, bytes_accessed=8 * 2**20, transcendentals=0),
            name="synthesis",
        )(first, white_noise, mode_amplitude, tables)

        chunk = depth * rows_y
        field = lax.all_to_all(
            sent.reshape(devices, chunk, BLOCK), ("px", "py"), split_axis=0, concat_axis=0, tiled=True
        )

        spread = spread_ranks(galaxy_in, keep, heavy, col_index)
        outgoing = jnp.concatenate([galaxy_in[::-1, :keep], spread[::-1]], axis=1)
        outgoing, field = lax.optimization_barrier((outgoing, field))
        counts = lax.all_to_all(
            outgoing,
            "py",
            split_axis=0,
            concat_axis=0,
            tiled=True,
            axis_index_groups=[list(range(rows_py - 1, -1, -1))],
        )

        cells = (size_z * rows_y, BLOCK)
        columns = span_x * span_y
        expected = pl.pallas_call(
            expected_kernel,
            out_shape=jax.ShapeDtypeStruct((size_z, columns), jnp.float32),
            compiler_params=pltpu.CompilerParams(vmem_limit_bytes=48 * 2**20),
            cost_estimate=pl.CostEstimate(
                flops=flops // 2, bytes_accessed=4 * 2**20, transcendentals=size_z * columns
            ),
            name="expected_counts",
        )(field.reshape(cells), bias_grid, density_grid, tables)
        inside = pl.BlockSpec(memory_space=pltpu.VMEM)
        back = pl.pallas_call(
            gradient_kernel,
            in_specs=[scalar, inside, inside, pl.BlockSpec(memory_space=pl.ANY), inside],
            out_shape=jax.ShapeDtypeStruct(cells, jnp.float32),
            scratch_shapes=[
                pltpu.VMEM((quarters * columns, BLOCK), counts.dtype),
                pltpu.VMEM(expected.shape, jnp.float32),
                pltpu.SemaphoreType.DMA,
            ],
            compiler_params=pltpu.CompilerParams(vmem_limit_bytes=56 * 2**20),
            cost_estimate=pl.CostEstimate(flops=flops // 2, bytes_accessed=8 * 2**20, transcendentals=0),
            name="shell_gradient",
        )(slot_grid.reshape(-1), counts.reshape(-1, BLOCK), bias_grid, expected, tables)

        returned = lax.all_to_all(
            back.reshape(devices, chunk, BLOCK), ("px", "py"), split_axis=0, concat_axis=0, tiled=True
        )
        step_size = adapted_step(accepted)
        steps = jnp.stack([step_size, jnp.sqrt(2.0 * step_size)])
        out_plane = jax.ShapeDtypeStruct(white_noise.shape, jnp.float32)
        return pl.pallas_call(
            analysis_kernel,
            grid=(depth,),
            in_specs=[scalar, scalar, packed, plane, plane, plane, whole(tables)],
            out_specs=(plane, plane),
            out_shape=(out_plane, out_plane),
            scratch_shapes=[tiled],
            compiler_params=pltpu.CompilerParams(vmem_limit_bytes=50 * 2**20),
            cost_estimate=pl.CostEstimate(flops=flops, bytes_accessed=12 * 2**20, transcendentals=0),
            name="analysis",
        )(first, steps, returned.reshape(packed_shape), white_noise, mode_amplitude, kick_noise, tables)

    modes = P(("px", "py"), None, None)
    return jax.shard_map(
        body,
        mesh=mesh,
        in_specs=(modes, modes, modes, P("px", "py", None), P("px", "py", None, None, None), P(), P(), P()),
        out_specs=(modes, modes),
        check_vma=False,
    )
```

```python
import math

import jax
import jax.numpy as jnp
import numpy as np
from jax import lax
from jax.experimental import pallas as pl
from jax.experimental.pallas import tpu as pltpu
from jax.sharding import PartitionSpec as P

BLOCK = 128
HALF = BLOCK // 2
WIDTH = 4
ROWS = 8
GROUP = 128
VMEM_BYTES = 56 * 1024 * 1024


def half_tables(order):
    place = np.arange(order // 2)
    parts = []
    for rows in (2 * place, 2 * place + 1):
        angle = (rows[:, None] * place[None, :] % order).astype(np.float64) * (2.0 * math.pi / order)
        parts.append(((np.cos(angle) + np.sin(angle)) / math.sqrt(order)).astype(np.float32))
    parts.append(parts[1].T)
    pairs = []
    for part in parts:
        high = part.astype(jnp.bfloat16)
        pairs += [high, (part - high.astype(np.float32)).astype(jnp.bfloat16)]
    return np.stack(pairs)


def split(value):
    high = value.astype(jnp.bfloat16)
    low = (value - high.astype(jnp.float32)).astype(jnp.bfloat16)
    return high, low


def product(left, right, contract=((1,), (0,))):
    left_high, left_low = left
    right_high, right_low = right
    dot = lambda a, b: lax.dot_general(a, b, (contract, ((), ())), preferred_element_type=jnp.float32)
    return dot(left_high, right_high) + (dot(left_high, right_low) + dot(left_low, right_high))


def first_half(shape):
    return lax.broadcasted_iota(jnp.int32, shape, len(shape) - 1) % BLOCK < HALF


def swap_halves(value):
    return pltpu.roll(value, HALF, axis=1)


def live_amplitude(first, amplitude):
    amplitude = amplitude.astype(jnp.float32)
    top = amplitude[:ROWS]
    rows = lax.broadcasted_iota(jnp.int32, top.shape, 0)
    cols = lax.broadcasted_iota(jnp.int32, top.shape, 1)
    top = jnp.where(rows + cols + first == 0, 0.0, top)
    return jnp.concatenate([top, amplitude[ROWS:]], axis=0)


def table_pairs(tables_ref):
    return [(tables_ref[2 * n], tables_ref[2 * n + 1]) for n in range(3)]


def fold(value, axis):
    left, right = jnp.split(value, 2, axis=axis)
    return left + right, left - right


def unfold(even, odd, axis):
    return jnp.concatenate([even + odd, even - odd], axis=axis)


def synthesis_kernel(first_ref, white_ref, amplitude_ref, tables_ref, out_ref, weighted_ref):
    even_table, odd_table, _ = table_pairs(tables_ref)
    tiles, size, _ = weighted_ref.shape
    weighted = live_amplitude(first_ref[0] + pl.program_id(0), amplitude_ref[0]) * white_ref[0]
    for tile in range(tiles):
        weighted_ref[tile] = weighted[:, tile * BLOCK : (tile + 1) * BLOCK]
    transposed = ((1,), (1,))
    passed = []
    for parity in range(2):
        rows = [weighted_ref[tile, pl.ds(parity, size // 2, stride=2), :] for tile in range(tiles)]
        total, change = fold(jnp.concatenate(rows, axis=1), 1)
        passed.append(
            (product(even_table, split(total), transposed), product(odd_table, split(change), transposed))
        )
    lower, upper = (
        unfold(product(split(passed[0][k]), even_table), product(split(passed[1][k]), odd_table), 1)
        for k in range(2)
    )
    groups = out_ref.shape[1]
    for pair in range(out_ref.shape[0] // 2):
        left = lower[:, pair * BLOCK : (pair + 1) * BLOCK]
        right = swap_halves(upper[:, pair * BLOCK : (pair + 1) * BLOCK])
        mask = first_half(left.shape)
        out_ref[2 * pair, :, 0] = jnp.where(mask, left, right).reshape(groups, -1, BLOCK)
        out_ref[2 * pair + 1, :, 0] = jnp.where(mask, right, left).reshape(groups, -1, BLOCK)


def expected_kernel(field_ref, bias_ref, density_ref, tables_ref, out_ref):
    even_table, _, odd_transposed = table_pairs(tables_ref)
    half_z = tables_ref.shape[1]
    rows_y = field_ref.shape[0] // (2 * half_z)
    for step in range(rows_y // 2):
        fields = [
            jnp.concatenate(
                [
                    field_ref[pl.ds(parity * rows_y + 2 * step + k, half_z, stride=2 * rows_y), :]
                    for k in range(2)
                ],
                axis=1,
            )
            for parity in range(2)
        ]
        contrast = unfold(product(even_table, split(fields[0])), product(odd_transposed, split(fields[1])), 0)
        span = slice(2 * step * BLOCK, 2 * (step + 1) * BLOCK)
        for quarter in range(2 * half_z // BLOCK):
            depth = slice(quarter * BLOCK, (quarter + 1) * BLOCK)
            bias = bias_ref[quarter : quarter + 1, span]
            density = density_ref[quarter : quarter + 1, span]
            out_ref[depth, span] = bias * (density * jnp.exp(bias * contrast[depth]))


def gradient_kernel(
    slot_ref, counts_ref, bias_ref, expected_any, tables_ref, out_ref, rows_ref, expected_ref, sem
):
    load = pltpu.make_async_copy(expected_any, expected_ref, sem)
    load.start()

    def gather(group, carry):
        base = pl.multiple_of(group * GROUP, GROUP)
        for k in range(GROUP):
            rows_ref[pl.ds(base + k, 1), :] = counts_ref[pl.ds(slot_ref[base + k], 1), :]
        return carry

    lax.fori_loop(0, rows_ref.shape[0] // GROUP, gather, 0)
    load.wait()
    even_table, odd_table, _ = table_pairs(tables_ref)
    half_z = tables_ref.shape[1]
    rows_y = out_ref.shape[0] // (2 * half_z)
    columns = expected_ref.shape[1]
    for step in range(rows_y // 2):
        span = slice(2 * step * BLOCK, 2 * (step + 1) * BLOCK)
        grads = []
        for quarter in range(2 * half_z // BLOCK):
            depth = slice(quarter * BLOCK, (quarter + 1) * BLOCK)
            starts = [quarter * columns + (2 * step + k) * BLOCK for k in range(2)]
            galaxy = jnp.concatenate(
                [rows_ref[start : start + BLOCK, :].astype(jnp.float32).T for start in starts], axis=1
            )
            grads.append(bias_ref[quarter : quarter + 1, span] * galaxy - expected_ref[depth, span])
        total, change = fold(jnp.concatenate(grads, axis=0), 0)
        for parity, back in enumerate([product(even_table, split(total)), product(odd_table, split(change))]):
            for k in range(2):
                row = pl.ds(parity * rows_y + 2 * step + k, half_z, stride=2 * rows_y)
                out_ref[row, :] = back[:, k * BLOCK : (k + 1) * BLOCK]


def analysis_kernel(
    first_ref, step_ref, field_ref, white_ref, amplitude_ref, kick_ref, tables_ref, grad_ref, next_ref, back_ref
):
    even_table, odd_table, _ = table_pairs(tables_ref)
    tiles, size, _ = back_ref.shape
    lower, upper = [], []
    for pair in range(field_ref.shape[0] // 2):
        left = field_ref[2 * pair, :, 0].reshape(-1, BLOCK)
        right = field_ref[2 * pair + 1, :, 0].reshape(-1, BLOCK)
        mask = first_half(left.shape)
        lower.append(jnp.where(mask, left, right))
        upper.append(swap_halves(jnp.where(mask, right, left)))
    transposed = ((1,), (1,))
    folded = [fold(jnp.concatenate(part, axis=1), 1) for part in (lower, upper)]
    for parity, table in enumerate([even_table, odd_table]):
        passed = [split(product(table, split(part[parity]), transposed)) for part in folded]
        back = unfold(product(passed[0], even_table), product(passed[1], odd_table), 1)
        for tile in range(tiles):
            rows = pl.ds(parity, size // 2, stride=2)
            back_ref[tile, rows, :] = back[:, tile * BLOCK : (tile + 1) * BLOCK]
    back = jnp.concatenate([back_ref[tile] for tile in range(tiles)], axis=1)
    white = white_ref[0]
    gradient = live_amplitude(first_ref[0] + pl.program_id(0), amplitude_ref[0]) * back - white
    grad_ref[0] = gradient
    next_ref[0] = white + step_ref[0] * gradient + step_ref[1] * kick_ref[0].astype(jnp.float32)


def adapted_step(accepted):
    powers = jnp.power(
        jnp.float32(0.9), jnp.arange(accepted.shape[0], dtype=jnp.int32).astype(jnp.float32)
    )
    accept_rate = jnp.float32(0.1) * jnp.sum(accepted.astype(jnp.float32) * powers)
    return jnp.float32(0.02) * jnp.exp(jnp.float32(2.0) * (accept_rate - jnp.float32(0.574)))


def spread_ranks(counts, keep, heavy, col_index):
    size, capacity, _ = counts.shape
    width = (capacity - keep) // WIDTH
    away = (col_index - heavy) % WIDTH
    part = lambda k: counts[:, keep + k * width : keep + (k + 1) * width]
    mine = part(0)
    for shift in range(1, WIDTH):
        pairs = [(i, i // WIDTH * WIDTH + (i + shift) % WIDTH) for i in range(size)]
        mine = jnp.where(away == shift, lax.ppermute(part(shift), "py", pairs), mine)
    return mine


def solution(mesh):
    rows_px, rows_py = mesh.shape["px"], mesh.shape["py"]
    devices = rows_px * rows_py

    def body(
        white_noise, mode_amplitude, kick_noise, shell_owner, galaxy_counts, shell_bias, shell_density, accepted
    ):
        depth, size_x, size_y = white_noise.shape
        size_z = depth * devices
        span_x, span_y = size_x // rows_px, size_y // rows_py
        rows_y = span_y // 2
        quarters = size_z // BLOCK
        row_index = lax.axis_index("px")
        col_index = lax.axis_index("py")
        first = ((row_index * rows_py + col_index) * depth).reshape(1)

        tables = jnp.asarray(half_tables(size_x))

        galaxy_in = galaxy_counts[0, 0]
        blocks, capacity = shell_owner.shape[-1], galaxy_counts.shape[3]
        keep = -(-(-(-(blocks - capacity) // (rows_py - 1))) // 8) * 8
        owner_list = shell_owner.reshape(-1)
        peers = jnp.arange(rows_py, dtype=jnp.int32)
        onehot = owner_list[:, None] == peers[None, :]
        onehot_int = onehot.astype(jnp.int32)
        rank_index = jnp.sum(jnp.cumsum(onehot_int, axis=0) * onehot_int, axis=1) - 1
        heavy = jnp.argmax(jnp.sum(onehot_int, axis=0)).astype(jnp.int32)
        width = (capacity - keep) // WIDTH
        place = rank_index - keep
        holder = owner_list // WIDTH * WIDTH + (owner_list + place // width) % WIDTH
        slot_index = jnp.where(
            place < 0,
            owner_list * (keep + width) + rank_index,
            holder * (keep + width) + keep + place % width,
        )
        bias_row = lax.dynamic_index_in_dim(shell_bias, row_index, 0, keepdims=False)
        density_row = lax.dynamic_index_in_dim(shell_density, row_index, 0, keepdims=False)

        def by_column(blocks):
            grid = blocks.reshape(span_x, rows_y, 2, quarters)
            grid = jnp.where(row_index % 2 == 0, grid, grid[:, :, ::-1])
            return grid.transpose(3, 1, 2, 0).reshape(quarters, -1)

        slot_grid = by_column(slot_index)
        owner_grid = by_column(owner_list)
        hit = owner_grid[:, :, None] == peers
        bias_grid = jnp.sum(jnp.where(hit, bias_row, 0.0), axis=-1)
        density_grid = jnp.sum(jnp.where(hit, density_row, 0.0), axis=-1)

        whole = lambda array: pl.BlockSpec(array.shape, lambda i: (0,) * array.ndim)
        plane = pl.BlockSpec((1, size_x, size_y), lambda i: (i, 0, 0))
        scalar = pl.BlockSpec(memory_space=pltpu.SMEM)
        packed_shape = (rows_px, rows_py, depth, rows_y, BLOCK)
        packed = pl.BlockSpec((rows_px, rows_py, 1, rows_y, BLOCK), lambda i: (0, 0, i, 0, 0))
        tiled = pltpu.VMEM((size_y // BLOCK, size_x, BLOCK), jnp.float32)
        params = pltpu.CompilerParams(vmem_limit_bytes=VMEM_BYTES)

        flops = 3 * 2 * depth * size_x * size_y * size_x
        sent = pl.pallas_call(
            synthesis_kernel,
            grid=(depth,),
            in_specs=[scalar, plane, plane, whole(tables)],
            out_specs=packed,
            scratch_shapes=[tiled],
            out_shape=jax.ShapeDtypeStruct(packed_shape, jnp.float32),
            compiler_params=params,
            cost_estimate=pl.CostEstimate(flops=flops, bytes_accessed=8 * 2**20, transcendentals=0),
            name="synthesis",
        )(first, white_noise, mode_amplitude, tables)

        chunk = depth * rows_y
        field = lax.all_to_all(
            sent.reshape(devices, chunk, BLOCK), ("px", "py"), split_axis=0, concat_axis=0, tiled=True
        )

        outgoing = jnp.concatenate([galaxy_in[:, :keep], spread_ranks(galaxy_in, keep, heavy, col_index)], axis=1)
        outgoing, field = lax.optimization_barrier((outgoing, field))
        counts = lax.all_to_all(outgoing, "py", split_axis=0, concat_axis=0, tiled=True)

        cells = (size_z * rows_y, BLOCK)
        columns = span_x * span_y
        expected = pl.pallas_call(
            expected_kernel,
            out_shape=jax.ShapeDtypeStruct((size_z, columns), jnp.float32),
            compiler_params=pltpu.CompilerParams(vmem_limit_bytes=48 * 2**20),
            cost_estimate=pl.CostEstimate(
                flops=flops // 2, bytes_accessed=4 * 2**20, transcendentals=size_z * columns
            ),
            name="expected_counts",
        )(field.reshape(cells), bias_grid, density_grid, tables)
        inside = pl.BlockSpec(memory_space=pltpu.VMEM)
        back = pl.pallas_call(
            gradient_kernel,
            in_specs=[scalar, inside, inside, pl.BlockSpec(memory_space=pl.ANY), inside],
            out_shape=jax.ShapeDtypeStruct(cells, jnp.float32),
            scratch_shapes=[
                pltpu.VMEM((quarters * columns, BLOCK), counts.dtype),
                pltpu.VMEM(expected.shape, jnp.float32),
                pltpu.SemaphoreType.DMA,
            ],
            compiler_params=pltpu.CompilerParams(vmem_limit_bytes=53 * 2**20),
            cost_estimate=pl.CostEstimate(flops=flops // 2, bytes_accessed=8 * 2**20, transcendentals=0),
            name="shell_gradient",
        )(slot_grid.reshape(-1), counts.reshape(-1, BLOCK), bias_grid, expected, tables)

        returned = lax.all_to_all(
            back.reshape(devices, chunk, BLOCK), ("px", "py"), split_axis=0, concat_axis=0, tiled=True
        )
        step_size = adapted_step(accepted)
        steps = jnp.stack([step_size, jnp.sqrt(2.0 * step_size)])
        out_plane = jax.ShapeDtypeStruct(white_noise.shape, jnp.float32)
        return pl.pallas_call(
            analysis_kernel,
            grid=(depth,),
            in_specs=[scalar, scalar, packed, plane, plane, plane, whole(tables)],
            out_specs=(plane, plane),
            out_shape=(out_plane, out_plane),
            scratch_shapes=[tiled],
            compiler_params=pltpu.CompilerParams(vmem_limit_bytes=50 * 2**20),
            cost_estimate=pl.CostEstimate(flops=flops, bytes_accessed=12 * 2**20, transcendentals=0),
            name="analysis",
        )(first, steps, returned.reshape(packed_shape), white_noise, mode_amplitude, kick_noise, tables)

    modes = P(("px", "py"), None, None)
    return jax.shard_map(
        body,
        mesh=mesh,
        in_specs=(modes, modes, modes, P("px", "py", None), P("px", "py", None, None, None), P(), P(), P()),
        out_specs=(modes, modes),
        check_vma=False,
    )
```
